1024 devices in a mesh: node: 64 (over x, y, core), local: 16 (over z).
Axes of the slice: x: 4, y: 8, z: 16, core: 2. Of those that a mesh axis runs over, the one named last changes fastest.
Arguments:
- grad_out: bfloat16 [8192, 3584], P('node', 'local'), may hold values from -6 to 6
- expert_ids: int32 [8192, 8], P('node'), may hold values from 0 to 255, as said below
- gate_scores: float32 [8192, 8], P('node'), may hold values from 0.05 to 0.95
- saved_hidden: bfloat16 [64, 512, 4096], P('node', None, 'local'), may hold values from -0.625 to 0.625
- down_weight: bfloat16 [262144, 3584], P(('node', 'local')), may hold values from -0.1875 to 0.1875
- shared_weight: bfloat16 [2048, 3584], P(None, 'local'), may hold values from -0.125 to 0.125
Outputs:
- expert_grad: bfloat16 [64, 512, 4096], P('node', None, 'local')
- router_grad: float32 [8192, 8], P('node')
- shared_grad: bfloat16 [2048, 8192], P('local', 'node')
The draws below stay inside these ranges and needn't reach their ends.
Inputs may be any that keep to these rules, and one draw needn't show every extreme that they name: `expert_ids`: each token names 8 different experts lying in exactly 4 different groups, at least one pick in each of them. Of the 128 tokens of one index of node, exactly 8 name each group.
All inputs are finite; a program needn't handle non-finite values.
Results may differ from the reference program's by a relative error of at most 0.0049.
Values may be sent and summed in bfloat16 or wider, within the bound.
No kernel may reach another device: no remote copies, remote signals or barrier semaphores. Data moves between devices by JAX's collectives and lax.ppermute only.
A program may use at most 32 MiB of HBM per device.

```python
import jax
import jax.numpy as jnp
from jax import lax

D = 3584
HID = 1024
SHARED = 2048
EXP_NODE = 4
TOP = 8
NODE_LIMIT = 4
TOK_NODE = 128
EXPERTS = 256
CAP = 8
TOKENS = 8192
N_NODE = 64


def draw_expert_ids(key, part):
    key = jax.random.fold_in(key, 11)
    key_nodes, key_tokens, key_hot, key_coin, key_free, key_extra = jax.random.split(key, 6)
    node_perm = jax.vmap(lambda sub: jax.random.permutation(sub, N_NODE))(jax.random.split(key_nodes, N_NODE))
    token_perm = jax.vmap(lambda sub: jax.random.permutation(sub, TOK_NODE))(jax.random.split(key_tokens, N_NODE))
    offsets = jnp.arange(NODE_LIMIT, dtype=jnp.int32) * (N_NODE // NODE_LIMIT)
    position = (token_perm[:, :, None] + offsets[None, None, :]) % N_NODE
    nodes = jax.vmap(lambda table, where_at: table[where_at])(node_perm, position)
    hot_expert = jax.random.randint(key_hot, (N_NODE,), 0, EXP_NODE)
    coin_flip = jax.random.randint(key_coin, (N_NODE, TOK_NODE, NODE_LIMIT), 0, 2)
    free_pick = jax.random.randint(key_free, (N_NODE, TOK_NODE, NODE_LIMIT), 0, EXP_NODE)
    first_pick = jnp.where(coin_flip == 0, hot_expert[nodes], free_pick)
    spare = NODE_LIMIT * (EXP_NODE - 1)
    extra_keys = jax.random.split(key_extra, N_NODE * TOK_NODE)
    chosen = jax.vmap(lambda sub: jax.random.permutation(sub, spare)[:NODE_LIMIT])(extra_keys)
    chosen = chosen.reshape(N_NODE, TOK_NODE, NODE_LIMIT).astype(jnp.int32)
    which_group = chosen // (EXP_NODE - 1)
    step_over = chosen % (EXP_NODE - 1) + 1
    extra_node = jnp.take_along_axis(nodes, which_group, axis=2)
    extra_pick = (jnp.take_along_axis(first_pick, which_group, axis=2) + step_over) % EXP_NODE
    picked = jnp.concatenate([nodes * EXP_NODE + first_pick, extra_node * EXP_NODE + extra_pick], axis=2)
    return picked.reshape(TOKENS, TOP).astype(jnp.int32)


def levels(key, extent, shards, least, largest):
    loudness = 1.0
    for dim, shards_of in shards:
        steps = jax.random.uniform(jax.random.fold_in(jax.random.fold_in(key, 6), dim), (shards_of,), jnp.float32, least / len(shards), largest / len(shards))
        loudness = loudness * jnp.repeat(jnp.exp(steps), extent[dim] // shards_of).reshape((-1,) + (1,) * (len(extent) - 1 - dim))
    return loudness


def normal_values(rng, shape, scale, limit, pieces=(), held_as=jnp.bfloat16):
    level = levels(rng, shape, pieces, -0.22, 0.18) if pieces else 1.0
    array = jax.random.normal(rng, shape, jnp.float32) * scale * level
    return jnp.minimum(jnp.maximum(array, -limit), limit).astype(held_as)


def setup_inputs(seed: int = 0) -> dict:
    streams_of = jax.random.split(jax.random.key(seed), 7)
    return {
        "grad_out": normal_values(streams_of[0], (TOKENS, D), 1.0, 6.0, ((0, 64), (1, 16))),
        "expert_ids": draw_expert_ids(jax.random.fold_in(streams_of[6], 71), 0),
        "gate_scores": jnp.clip(0.05 + 0.9 * jax.random.uniform(streams_of[2], (TOKENS, TOP), jnp.float32) ** levels(streams_of[2], (TOKENS, TOP), ((0, 64),), -0.2, 0.2), 0.05, 0.95),
        "saved_hidden": normal_values(streams_of[3], (N_NODE, N_NODE * CAP, EXP_NODE * HID), 0.1, 0.625, ((0, 64), (2, 16))),
        "down_weight": normal_values(streams_of[4], (EXPERTS * HID, D), HID ** -0.5, 0.1875, ((0, 1024),)),
        "shared_weight": normal_values(streams_of[5], (SHARED, D), SHARED ** -0.5, 0.125, ((1, 16),)),
    }


route_scale = 2.5


def reference(grad_out, expert_ids, gate_scores, saved_hidden, down_weight, shared_weight):
    node_ids = expert_ids // EXP_NODE
    local_ids = expert_ids % EXP_NODE
    groups = jnp.arange(N_NODE, dtype=jnp.int32)
    node_hits = jnp.any(node_ids[:, :, None] == groups[None, None, :], axis=1).astype(jnp.int32)
    slot_index = (jnp.cumsum(node_hits.reshape(N_NODE, TOK_NODE, N_NODE), axis=1) - 1).reshape(TOKENS, N_NODE)
    source = jnp.arange(TOKENS, dtype=jnp.int32) // TOK_NODE
    totals = jnp.sum(gate_scores, axis=1, keepdims=True)
    weights = route_scale * gate_scores / totals
    weights_low = lax.optimization_barrier(weights.astype(jnp.bfloat16))
    weights_sent = weights_low.astype(jnp.float32)
    pick_slot = jnp.take_along_axis(slot_index, node_ids, axis=1)
    pick_row = (source[:, None] * CAP + pick_slot).astype(jnp.int32)
    rows_total = N_NODE * CAP

    def one_group(inputs):
        group, hidden_group = inputs
        in_group = node_hits[:, group] == 1
        token_row = jnp.where(in_group, source * CAP + slot_index[:, group], rows_total).astype(jnp.int32)
        dispatched = jnp.zeros((rows_total, D), jnp.bfloat16).at[token_row].set(grad_out, mode="drop")
        gate_rows = jnp.where(node_ids == group, pick_row, rows_total).astype(jnp.int32)
        gate_table = jnp.zeros((rows_total, EXP_NODE), jnp.float32).at[gate_rows, local_ids].set(weights_sent, mode="drop")
        outputs = []
        scores = []
        for column in range(EXP_NODE):
            first_row = ((group * EXP_NODE + column) * HID).astype(jnp.int32)
            block = lax.dynamic_slice_in_dim(down_weight, first_row, HID, 0)
            hidden_grad = lax.dot_general(dispatched, block, (((1,), (1,)), ((), ())), preferred_element_type=jnp.float32)
            saved = hidden_group[:, column * HID:(column + 1) * HID].astype(jnp.float32)
            scores.append(jnp.sum(hidden_grad * saved, axis=1))
            outputs.append((gate_table[:, column:column + 1] * hidden_grad).astype(jnp.bfloat16))
        return jnp.concatenate(outputs, axis=1), jnp.stack(scores, axis=1)

    expert_grad, slot_score = lax.map(one_group, (groups, saved_hidden))
    contrib = slot_score[node_ids, pick_row, local_ids]
    mean_term = jnp.sum(gate_scores * contrib, axis=1, keepdims=True) / totals
    router_grad = route_scale / totals * (contrib - mean_term) * gate_scores * (1.0 - gate_scores)
    shared_grad = lax.dot_general(shared_weight, grad_out, (((1,), (1,)), ((), ())), preferred_element_type=jnp.float32).astype(jnp.bfloat16)
    return expert_grad, router_grad, shared_grad
```

```python
import jax
import jax.numpy as jnp
from jax import lax
from jax.experimental import pallas as pl
from jax.experimental.pallas import tpu as pltpu
from jax.sharding import PartitionSpec as P

EXP_NODE = 4
LANES = 128

route_scale = 2.5


def iota(shape, dim):
    return lax.broadcasted_iota(jnp.int32, shape, dim)


def route_kernel(capacity, grad_ref, ids_ref, scores_ref, payload_ref, select_ref, wide_ref):
    tokens, width = grad_ref.shape
    rows, padded = payload_ref.shape
    top = ids_ref.shape[1]
    experts = rows // capacity * EXP_NODE
    ids = ids_ref[...]
    scores = scores_ref[...]
    group = iota((tokens, rows), 1) // capacity
    hits = group == ids[:, 0:1] // EXP_NODE
    for k in range(1, top):
        hits = hits | (group == ids[:, k:k + 1] // EXP_NODE)
    before = (iota((tokens, tokens), 1) < iota((tokens, tokens), 0)).astype(jnp.float32).astype(jnp.bfloat16)
    hot = hits.astype(jnp.float32)
    rank = jnp.dot(before, hot.astype(jnp.bfloat16), preferred_element_type=jnp.float32)
    slot = (iota((tokens, rows), 1) % capacity).astype(jnp.float32)
    select = jnp.where(rank == slot, hot, 0.0).astype(jnp.bfloat16)
    select_ref[...] = select
    totals = jnp.sum(scores, axis=1, keepdims=True)
    weights = (route_scale * scores / totals).astype(jnp.bfloat16).astype(jnp.float32)
    expert = iota((tokens, experts), 1)
    spread = jnp.zeros((tokens, experts), jnp.float32)
    for k in range(top):
        spread = spread + jnp.where(expert == ids[:, k:k + 1], weights[:, k:k + 1], 0.0)
    wide_ref[...] = jnp.zeros(wide_ref.shape, wide_ref.dtype)
    wide_ref[:, :width] = grad_ref[...]
    across = (((0,), (0,)), ((), ()))
    sent = lax.dot_general(select, wide_ref[...], across, preferred_element_type=jnp.float32)
    gates = lax.dot_general(
        select, spread.astype(jnp.bfloat16), across, preferred_element_type=jnp.float32
    )
    own = iota((rows, experts), 0) // capacity == iota((rows, experts), 1) // EXP_NODE
    place = iota((experts, padded), 0) % EXP_NODE + width == iota((experts, padded), 1)
    gates = jnp.dot(
        jnp.where(own, gates, 0.0).astype(jnp.bfloat16),
        place.astype(jnp.float32).astype(jnp.bfloat16),
        preferred_element_type=jnp.float32,
    )
    payload_ref[...] = (sent + gates).astype(payload_ref.dtype)


def router_kernel(capacity, parts_ref, select_ref, ids_ref, scores_ref, out_ref):
    tokens, rows = select_ref.shape
    top = ids_ref.shape[1]
    groups = rows // capacity
    shares = parts_ref.shape[0] // EXP_NODE
    ids = ids_ref[...]
    scores = scores_ref[...]
    select = select_ref[...].astype(jnp.float32)
    fold = (iota((rows, groups), 0) // capacity == iota((rows, groups), 1)).astype(jnp.float32)
    first = iota((tokens, groups), 1) * EXP_NODE
    columns = []
    for c in range(EXP_NODE):
        score = jnp.sum(parts_ref[c * shares:(c + 1) * shares, :], axis=0, keepdims=True)
        columns.append(
            jnp.dot(select * score, fold, precision=lax.Precision.HIGHEST, preferred_element_type=jnp.float32)
        )
    pick = iota((tokens, top), 1)
    contrib = jnp.zeros((tokens, top), jnp.float32)
    for k in range(top):
        value = jnp.zeros((tokens, groups), jnp.float32)
        for c in range(EXP_NODE):
            value = value + jnp.where(first + c == ids[:, k:k + 1], columns[c], 0.0)
        contrib = contrib + jnp.where(pick == k, jnp.sum(value, axis=1, keepdims=True), 0.0)
    totals = jnp.sum(scores, axis=1, keepdims=True)
    mean_term = jnp.sum(scores * contrib, axis=1, keepdims=True) / totals
    out_ref[...] = route_scale / totals * (contrib - mean_term) * scores * (1.0 - scores)


def body(grad_out, expert_ids, gate_scores, saved_hidden, down_weight, shared_weight):
    node_count = lax.axis_size("node")
    local_count = lax.axis_size("local")
    rows_total = saved_hidden.shape[1]
    capacity = rows_total // node_count
    tokens, slice_width = grad_out.shape
    quarter_width = down_weight.shape[0]
    share_count = local_count // EXP_NODE
    padded = (slice_width + EXP_NODE + LANES - 1) // LANES * LANES
    own_expert = lax.axis_index("local") // share_count

    payload, select = pl.pallas_call(
        lambda *refs: route_kernel(capacity, *refs),
        out_shape=(
            jax.ShapeDtypeStruct((rows_total, padded), jnp.bfloat16),
            jax.ShapeDtypeStruct((tokens, rows_total), jnp.bfloat16),
        ),
        scratch_shapes=[pltpu.VMEM((tokens, padded), jnp.bfloat16)],
    )(grad_out, expert_ids, gate_scores)
    received = lax.all_to_all(
        payload.reshape(node_count, capacity, padded), "node", split_axis=0, concat_axis=0, tiled=True
    ).reshape(rows_total, padded)

    own_rows = received[:, :slice_width].T
    full_rows = lax.all_gather(own_rows, "local", axis=0, tiled=True)

    shared_part = lax.dot_general(
        shared_weight, grad_out, (((1,), (1,)), ((), ())), preferred_element_type=jnp.float32
    ).astype(jnp.bfloat16)
    shared_part, _ = lax.optimization_barrier((shared_part, received))
    shared_parts = lax.all_to_all(
        shared_part.reshape(local_count, -1, tokens), "local", split_axis=0, concat_axis=0, tiled=True
    )
    shared_grad = jnp.sum(shared_parts.astype(jnp.float32), axis=0).astype(jnp.bfloat16)

    hidden_grad = lax.dot_general(
        full_rows, down_weight, (((0,), (1,)), ((), ())), preferred_element_type=jnp.float32
    )
    gate_column = lax.dynamic_slice_in_dim(received, slice_width + own_expert, 1, 1).astype(jnp.float32)
    expert_grad = (
        (gate_column * hidden_grad).astype(jnp.bfloat16).reshape(1, rows_total, quarter_width)
    )
    slot_dots = jnp.sum(hidden_grad * saved_hidden[0].astype(jnp.float32), axis=1)

    returned = lax.all_to_all(
        slot_dots.reshape(node_count, 1, capacity), "node", split_axis=0, concat_axis=0, tiled=True
    )
    spread = jnp.broadcast_to(
        returned.reshape(1, rows_total // LANES, LANES), (local_count, rows_total // LANES, LANES)
    )
    parts = lax.all_to_all(spread, "local", split_axis=0, concat_axis=0, tiled=True)
    router_grad = pl.pallas_call(
        lambda *refs: router_kernel(capacity, *refs),
        out_shape=jax.ShapeDtypeStruct(gate_scores.shape, jnp.float32),
    )(parts.reshape(local_count, rows_total), select, expert_ids, gate_scores)
    return (expert_grad, router_grad, shared_grad)


def solution(mesh):
    return jax.shard_map(
        body,
        mesh=mesh,
        in_specs=(
            P("node", "local"),
            P("node", None),
            P("node", None),
            P("node", None, "local"),
            P(("node", "local"), None),
            P(None, "local"),
        ),
        out_specs=(P("node", None, "local"), P("node", None), P("local", "node")),
        check_vma=False,
    )
```

```python
import jax
import jax.numpy as jnp
from jax import lax
from jax.experimental import pallas as pl
from jax.experimental.pallas import tpu as pltpu
from jax.sharding import PartitionSpec as P

EXP_NODE = 4
LANES = 128

route_scale = 2.5


def iota(shape, dim):
    return lax.broadcasted_iota(jnp.int32, shape, dim)


def as_bf16(mask):
    return mask.astype(jnp.float32).astype(jnp.bfloat16)


def across(left, right):
    return lax.dot_general(left, right, (((1,), (1,)), ((), ())), preferred_element_type=jnp.float32)


def exact_dot(left, right):
    high = left.astype(jnp.bfloat16)
    rest = left - high.astype(jnp.float32)
    middle = rest.astype(jnp.bfloat16)
    low = (rest - middle.astype(jnp.float32)).astype(jnp.bfloat16)
    return (
        jnp.dot(high, right, preferred_element_type=jnp.float32)
        + jnp.dot(middle, right, preferred_element_type=jnp.float32)
        + jnp.dot(low, right, preferred_element_type=jnp.float32)
    )


def route_kernel(capacity, grad_ref, ids_ref, scores_ref, payload_ref, select_ref, wide_ref):
    width, tokens = grad_ref.shape
    rows, padded = payload_ref.shape
    top = ids_ref.shape[0]
    experts = rows // capacity * EXP_NODE
    ids = ids_ref[...]
    scores = scores_ref[...]
    wide_ref[...] = jnp.zeros(wide_ref.shape, wide_ref.dtype)
    wide_ref[:width, :] = grad_ref[...]
    group = iota((rows, tokens), 0) // capacity
    picked = ids // EXP_NODE
    hits = group == picked[0:1, :]
    for k in range(1, top):
        hits = hits | (group == picked[k:k + 1, :])
    hot = hits.astype(jnp.float32)
    before = as_bf16(iota((tokens, tokens), 0) < iota((tokens, tokens), 1))
    rank = jnp.dot(hot.astype(jnp.bfloat16), before, preferred_element_type=jnp.float32)
    slot = (iota((rows, tokens), 0) % capacity).astype(jnp.float32)
    select = jnp.where(rank == slot, hot, 0.0).astype(jnp.bfloat16)
    select_ref[...] = select
    totals = jnp.sum(scores, axis=0, keepdims=True)
    weights = (route_scale * scores / totals).astype(jnp.bfloat16).astype(jnp.float32)
    expert = iota((experts, tokens), 0)
    spread = jnp.zeros((experts, tokens), jnp.float32)
    for k in range(top):
        spread = spread + jnp.where(expert == ids[k:k + 1, :], weights[k:k + 1, :], 0.0)
    sent = across(select, wide_ref[...])
    gates = across(select, spread.astype(jnp.bfloat16))
    own = iota((rows, experts), 0) // capacity == iota((rows, experts), 1) // EXP_NODE
    place = iota((experts, padded), 0) % EXP_NODE + width == iota((experts, padded), 1)
    gates = jnp.dot(
        jnp.where(own, gates, 0.0).astype(jnp.bfloat16), as_bf16(place), preferred_element_type=jnp.float32
    )
    payload_ref[...] = (sent + gates).astype(payload_ref.dtype)


def spread_kernel(capacity, score_ref, out_ref):
    groups = score_ref.shape[0]
    copies, lines, lanes = out_ref.shape
    score = score_ref[...].reshape(groups, score_ref.shape[2])
    held = lanes // capacity
    repeat = as_bf16(iota((capacity, lanes), 0) == iota((capacity, lanes), 1) % capacity)
    tiled = exact_dot(score, repeat)
    tiled = jnp.where(iota((groups, lanes), 0) % held == iota((groups, lanes), 1) // capacity, tiled, 0.0)
    flat = jnp.concatenate(
        [jnp.sum(tiled[j * held:(j + 1) * held, :], axis=0, keepdims=True) for j in range(lines)], axis=0
    )
    for z in range(copies):
        out_ref[z] = flat


def router_kernel(capacity, parts_ref, select_ref, ids_ref, scores_ref, out_ref):
    copies, lines, lanes = parts_ref.shape
    rows, tokens = select_ref.shape
    top = ids_ref.shape[0]
    shares = copies // EXP_NODE
    held = lanes // capacity
    ids = ids_ref[...]
    scores = scores_ref[...]
    fold = iota((held, lanes), 0) == iota((held, lanes), 1) // capacity
    score = []
    for c in range(EXP_NODE):
        total = parts_ref[c * shares]
        for q in range(1, shares):
            total = total + parts_ref[c * shares + q]
        score.append(total)
    pick = iota((top, tokens), 0)
    line = iota((EXP_NODE * held, tokens), 0)
    expert = line % held * EXP_NODE + line // held
    contrib = jnp.zeros((top, tokens), jnp.float32)
    for j in range(lines):
        left = jnp.concatenate([jnp.where(fold, score[c][j:j + 1, :], 0.0) for c in range(EXP_NODE)], axis=0)
        found = exact_dot(left, select_ref[j * lanes:(j + 1) * lanes, :])
        for k in range(top):
            mine = jnp.where(expert + j * held * EXP_NODE == ids[k:k + 1, :], found, 0.0)
            contrib = contrib + jnp.where(pick == k, jnp.sum(mine, axis=0, keepdims=True), 0.0)
    totals = jnp.sum(scores, axis=0, keepdims=True)
    mean_term = jnp.sum(scores * contrib, axis=0, keepdims=True) / totals
    out_ref[...] = route_scale / totals * (contrib - mean_term) * scores * (1.0 - scores)


def body(grad_out, expert_ids, gate_scores, saved_hidden, down_weight, shared_weight):
    node_count = lax.axis_size("node")
    local_count = lax.axis_size("local")
    rows_total = saved_hidden.shape[1]
    capacity = rows_total // node_count
    tokens, slice_width = grad_out.shape
    quarter_width = down_weight.shape[0]
    share_count = local_count // EXP_NODE
    padded = (slice_width + EXP_NODE + LANES - 1) // LANES * LANES
    own_expert = lax.axis_index("local") // share_count
    ids = expert_ids.T
    scores = gate_scores.T

    payload, select = pl.pallas_call(
        lambda *refs: route_kernel(capacity, *refs),
        out_shape=(
            jax.ShapeDtypeStruct((rows_total, padded), jnp.bfloat16),
            jax.ShapeDtypeStruct((rows_total, tokens), jnp.bfloat16),
        ),
        scratch_shapes=[pltpu.VMEM((padded, tokens), jnp.bfloat16)],
    )(grad_out.T, ids, scores)
    received = lax.all_to_all(
        payload.reshape(node_count, capacity, padded), "node", split_axis=0, concat_axis=0, tiled=True
    ).reshape(rows_total, padded)

    own_rows = received[:, :slice_width].T
    full_rows = lax.all_gather(own_rows, "local", axis=0, tiled=True)

    shared_part = lax.dot_general(
        shared_weight, grad_out, (((1,), (1,)), ((), ())), preferred_element_type=jnp.float32
    ).astype(jnp.bfloat16)
    shared_part, _ = lax.optimization_barrier((shared_part, own_rows))
    shared_parts = lax.all_to_all(
        shared_part.reshape(local_count, -1, tokens), "local", split_axis=0, concat_axis=0, tiled=True
    )
    shared_grad = jnp.sum(shared_parts.astype(jnp.float32), axis=0).astype(jnp.bfloat16)
    full_rows, shared_grad = lax.optimization_barrier((full_rows, shared_grad))

    hidden_grad = lax.dot_general(
        full_rows, down_weight, (((0,), (1,)), ((), ())), preferred_element_type=jnp.float32
    )
    gate_column = lax.dynamic_slice_in_dim(received, slice_width + own_expert, 1, 1).astype(jnp.float32)
    expert_grad = (
        (gate_column * hidden_grad).astype(jnp.bfloat16).reshape(1, rows_total, quarter_width)
    )
    slot_dots = jnp.sum(hidden_grad * saved_hidden[0].astype(jnp.float32), axis=1)

    returned = lax.all_to_all(
        slot_dots.reshape(node_count, 1, capacity), "node", split_axis=0, concat_axis=0, tiled=True
    )
    spread = pl.pallas_call(
        lambda *refs: spread_kernel(capacity, *refs),
        out_shape=jax.ShapeDtypeStruct((local_count, rows_total // LANES, LANES), jnp.float32),
    )(returned)
    parts = lax.all_to_all(spread, "local", split_axis=0, concat_axis=0, tiled=True)
    router_grad = pl.pallas_call(
        lambda *refs: router_kernel(capacity, *refs),
        out_shape=jax.ShapeDtypeStruct(scores.shape, jnp.float32),
    )(parts, select, ids, scores)
    return (expert_grad, router_grad.T, shared_grad)


def solution(mesh):
    return jax.shard_map(
        body,
        mesh=mesh,
        in_specs=(
            P("node", "local"),
            P("node", None),
            P("node", None),
            P("node", None, "local"),
            P(("node", "local"), None),
            P(None, "local"),
        ),
        out_specs=(P("node", None, "local"), P("node", None), P("local", "node")),
        check_vma=False,
    )
```

```python
import jax
import jax.numpy as jnp
from jax import lax
from jax.experimental import pallas as pl
from jax.experimental.pallas import tpu as pltpu
from jax.sharding import PartitionSpec as P

EXP_NODE = 4
LANES = 128
CLASSES = 4

route_scale = 2.5


def iota(shape, dim):
    return lax.broadcasted_iota(jnp.int32, shape, dim)


def as_bf16(mask):
    return mask.astype(jnp.float32).astype(jnp.bfloat16)


def across(left, right):
    return lax.dot_general(left, right, (((1,), (1,)), ((), ())), preferred_element_type=jnp.float32)


def exact_dot(left, right):
    high = left.astype(jnp.bfloat16)
    rest = left - high.astype(jnp.float32)
    middle = rest.astype(jnp.bfloat16)
    low = (rest - middle.astype(jnp.float32)).astype(jnp.bfloat16)
    return (
        jnp.dot(high, right, preferred_element_type=jnp.float32)
        + jnp.dot(middle, right, preferred_element_type=jnp.float32)
        + jnp.dot(low, right, preferred_element_type=jnp.float32)
    )


def route_kernel(capacity, grad_ref, ids_ref, scores_ref, payload_ref, select_ref, wide_ref):
    width, tokens = grad_ref.shape
    rows, padded = payload_ref.shape
    top = ids_ref.shape[0]
    experts = rows // capacity * EXP_NODE
    ids = ids_ref[...]
    scores = scores_ref[...]
    wide_ref[...] = jnp.zeros(wide_ref.shape, wide_ref.dtype)
    wide_ref[:width, :] = grad_ref[...]
    group = iota((rows, tokens), 0) // capacity
    picked = ids // EXP_NODE
    hits = group == picked[0:1, :]
    for k in range(1, top):
        hits = hits | (group == picked[k:k + 1, :])
    hot = hits.astype(jnp.float32)
    before = as_bf16(iota((tokens, tokens), 0) < iota((tokens, tokens), 1))
    rank = jnp.dot(hot.astype(jnp.bfloat16), before, preferred_element_type=jnp.float32)
    slot = (iota((rows, tokens), 0) % capacity).astype(jnp.float32)
    select = jnp.where(rank == slot, hot, 0.0).astype(jnp.bfloat16)
    select_ref[...] = select
    totals = jnp.sum(scores, axis=0, keepdims=True)
    weights = (route_scale * scores / totals).astype(jnp.bfloat16).astype(jnp.float32)
    expert = iota((experts, tokens), 0)
    spread = jnp.zeros((experts, tokens), jnp.float32)
    for k in range(top):
        spread = spread + jnp.where(expert == ids[k:k + 1, :], weights[k:k + 1, :], 0.0)
    sent = across(select, wide_ref[...])
    gates = across(select, spread.astype(jnp.bfloat16))
    own = iota((rows, experts), 0) // capacity == iota((rows, experts), 1) // EXP_NODE
    place = iota((experts, padded), 0) % EXP_NODE + width == iota((experts, padded), 1)
    gates = jnp.dot(
        jnp.where(own, gates, 0.0).astype(jnp.bfloat16), as_bf16(place), preferred_element_type=jnp.float32
    )
    payload_ref[...] = (sent + gates).astype(payload_ref.dtype)


def spread_kernel(capacity, score_ref, out_ref):
    groups = score_ref.shape[0]
    copies, lines, lanes = out_ref.shape
    score = score_ref[...].reshape(groups, score_ref.shape[2])
    held = lanes // capacity
    repeat = as_bf16(iota((capacity, lanes), 0) == iota((capacity, lanes), 1) % capacity)
    tiled = exact_dot(score, repeat)
    tiled = jnp.where(iota((groups, lanes), 0) % held == iota((groups, lanes), 1) // capacity, tiled, 0.0)
    flat = jnp.concatenate(
        [jnp.sum(tiled[j * held:(j + 1) * held, :], axis=0, keepdims=True) for j in range(lines)], axis=0
    )
    for z in range(copies):
        out_ref[z] = flat


def router_kernel(capacity, parts_ref, select_ref, ids_ref, scores_ref, out_ref):
    copies, lines, lanes = parts_ref.shape
    rows, tokens = select_ref.shape
    top = ids_ref.shape[0]
    shares = copies // EXP_NODE
    held = lanes // capacity
    ids = ids_ref[...]
    scores = scores_ref[...]
    fold = iota((held, lanes), 0) == iota((held, lanes), 1) // capacity
    score = []
    for c in range(EXP_NODE):
        total = parts_ref[c * shares]
        for q in range(1, shares):
            total = total + parts_ref[c * shares + q]
        score.append(total)
    pick = iota((top, tokens), 0)
    line = iota((EXP_NODE * held, tokens), 0)
    expert = line % held * EXP_NODE + line // held
    contrib = jnp.zeros((top, tokens), jnp.float32)
    for j in range(lines):
        left = jnp.concatenate([jnp.where(fold, score[c][j:j + 1, :], 0.0) for c in range(EXP_NODE)], axis=0)
        found = exact_dot(left, select_ref[j * lanes:(j + 1) * lanes, :])
        for k in range(top):
            mine = jnp.where(expert + j * held * EXP_NODE == ids[k:k + 1, :], found, 0.0)
            contrib = contrib + jnp.where(pick == k, jnp.sum(mine, axis=0, keepdims=True), 0.0)
    totals = jnp.sum(scores, axis=0, keepdims=True)
    mean_term = jnp.sum(scores * contrib, axis=0, keepdims=True) / totals
    out_ref[...] = route_scale / totals * (contrib - mean_term) * scores * (1.0 - scores)


def body(grad_out, expert_ids, gate_scores, saved_hidden, down_weight, shared_weight):
    node_count = lax.axis_size("node")
    local_count = lax.axis_size("local")
    rows_total = saved_hidden.shape[1]
    capacity = rows_total // node_count
    tokens, slice_width = grad_out.shape
    quarter_width = down_weight.shape[0]
    share_count = local_count // EXP_NODE
    padded = (slice_width + EXP_NODE + LANES - 1) // LANES * LANES
    own_expert = lax.axis_index("local") // share_count
    ids = expert_ids.T
    scores = gate_scores.T

    payload, select = pl.pallas_call(
        lambda *refs: route_kernel(capacity, *refs),
        out_shape=(
            jax.ShapeDtypeStruct((rows_total, padded), jnp.bfloat16),
            jax.ShapeDtypeStruct((rows_total, tokens), jnp.bfloat16),
        ),
        scratch_shapes=[pltpu.VMEM((padded, tokens), jnp.bfloat16)],
    )(grad_out.T, ids, scores)
    shared_part = lax.dot_general(
        shared_weight, grad_out, (((1,), (1,)), ((), ())), preferred_element_type=jnp.float32
    )
    payload, shared_part = lax.optimization_barrier((payload, shared_part))
    shared_grad = lax.psum_scatter(shared_part, "local", scatter_dimension=0, tiled=True).astype(jnp.bfloat16)
    received = lax.all_to_all(
        payload.reshape(node_count, capacity, padded), "node", split_axis=0, concat_axis=0, tiled=True
    ).reshape(rows_total, padded)

    own_rows = received[:, :slice_width].T
    groups = [list(range(j, local_count, CLASSES)) for j in range(CLASSES)]
    held = lax.all_gather(own_rows, "local", axis=0, tiled=True, axis_index_groups=groups)
    half = held.shape[0] // 2
    lower, upper = held[:half], held[half:]
    right = [(z, (z + 1) % local_count) for z in range(local_count)]
    left = [(z, (z - 1) % local_count) for z in range(local_count)]
    lower_left = lax.ppermute(lower, "local", right)
    upper_right = lax.ppermute(upper, "local", left)
    upper_left = lax.ppermute(upper, "local", right)
    lower_right = lax.ppermute(lower, "local", left)
    lower_far = lax.ppermute(lower_left, "local", right)
    upper_far = lax.ppermute(upper_right, "local", left)

    by_class = down_weight.reshape(quarter_width, 2, -1, CLASSES, slice_width)
    by_class = by_class.transpose(3, 1, 0, 2, 4).reshape(CLASSES, 2, quarter_width, half)

    def partial(rows, shift, part):
        own_class = (lax.axis_index("local") + shift) % CLASSES
        weight = lax.dynamic_index_in_dim(by_class, own_class, 0, keepdims=False)[part]
        return lax.dot_general(rows, weight, (((0,), (1,)), ((), ())), preferred_element_type=jnp.float32)

    hidden_grad = partial(lower, 0, 0) + partial(upper, 0, 1)
    hidden_grad = hidden_grad + partial(lower_left, CLASSES - 1, 0)
    hidden_grad = hidden_grad + partial(upper_right, 1, 1)
    hidden_grad = hidden_grad + partial(upper_left, CLASSES - 1, 1)
    hidden_grad = hidden_grad + partial(lower_right, 1, 0)
    hidden_grad = hidden_grad + partial(lower_far, 2, 0)
    hidden_grad = hidden_grad + partial(upper_far, 2, 1)
    gate_column = lax.dynamic_slice_in_dim(received, slice_width + own_expert, 1, 1).astype(jnp.float32)
    expert_grad = (
        (gate_column * hidden_grad).astype(jnp.bfloat16).reshape(1, rows_total, quarter_width)
    )
    slot_dots = jnp.sum(hidden_grad * saved_hidden[0].astype(jnp.float32), axis=1)

    returned = lax.all_to_all(
        slot_dots.reshape(node_count, 1, capacity), "node", split_axis=0, concat_axis=0, tiled=True
    )
    spread = pl.pallas_call(
        lambda *refs: spread_kernel(capacity, *refs),
        out_shape=jax.ShapeDtypeStruct((local_count, rows_total // LANES, LANES), jnp.float32),
    )(returned)
    parts = lax.all_to_all(spread, "local", split_axis=0, concat_axis=0, tiled=True)
    router_grad = pl.pallas_call(
        lambda *refs: router_kernel(capacity, *refs),
        out_shape=jax.ShapeDtypeStruct(scores.shape, jnp.float32),
    )(parts, select, ids, scores)
    return (expert_grad, router_grad.T, shared_grad)


def solution(mesh):
    return jax.shard_map(
        body,
        mesh=mesh,
        in_specs=(
            P("node", "local"),
            P("node", None),
            P("node", None),
            P("node", None, "local"),
            P(("node", "local"), None),
            P(None, "local"),
        ),
        out_specs=(P("node", None, "local"), P("node", None), P("local", "node")),
        check_vma=False,
    )
```

```python
import jax
import jax.numpy as jnp
from jax import lax
from jax.experimental import pallas as pl
from jax.experimental.pallas import tpu as pltpu
from jax.sharding import PartitionSpec as P

EXP_NODE = 4
LANES = 128
CLASSES = 4
KERNEL_VMEM = 8 << 20

route_scale = 2.5


def iota(shape, dim):
    return lax.broadcasted_iota(jnp.int32, shape, dim)


def as_bf16(mask):
    return mask.astype(jnp.float32).astype(jnp.bfloat16)


def across(left, right):
    return lax.dot_general(left, right, (((1,), (1,)), ((), ())), preferred_element_type=jnp.float32)


def pieces(value):
    high = value.astype(jnp.bfloat16)
    rest = value - high.astype(jnp.float32)
    middle = rest.astype(jnp.bfloat16)
    low = (rest - middle.astype(jnp.float32)).astype(jnp.bfloat16)
    return high, middle, low


def exact_dot(left, right):
    high, middle, low = (jnp.dot(piece, right, preferred_element_type=jnp.float32) for piece in pieces(left))
    return high + middle + low


def route_kernel(capacity, grad_ref, ids_ref, scores_ref, payload_ref, select_ref, wide_ref):
    width, tokens = grad_ref.shape
    rows, padded = payload_ref.shape
    top = ids_ref.shape[0]
    experts = rows // capacity * EXP_NODE
    ids = ids_ref[...]
    scores = scores_ref[...]
    wide_ref[...] = jnp.zeros(wide_ref.shape, wide_ref.dtype)
    wide_ref[:width, :] = grad_ref[...]
    group = iota((rows, tokens), 0) // capacity
    picked = ids // EXP_NODE
    hits = group == picked[0:1, :]
    for k in range(1, top):
        hits = hits | (group == picked[k:k + 1, :])
    hot = hits.astype(jnp.float32)
    before = as_bf16(iota((tokens, tokens), 0) < iota((tokens, tokens), 1))
    rank = jnp.dot(hot.astype(jnp.bfloat16), before, preferred_element_type=jnp.float32)
    slot = (iota((rows, tokens), 0) % capacity).astype(jnp.float32)
    select = jnp.where(rank == slot, hot, 0.0).astype(jnp.bfloat16)
    select_ref[...] = select
    totals = jnp.sum(scores, axis=0, keepdims=True)
    weights = (route_scale * scores / totals).astype(jnp.bfloat16).astype(jnp.float32)
    expert = iota((experts, tokens), 0)
    spread = jnp.zeros((experts, tokens), jnp.float32)
    for k in range(top):
        spread = spread + jnp.where(expert == ids[k:k + 1, :], weights[k:k + 1, :], 0.0)
    sent = across(select, wide_ref[...])
    gates = across(select, spread.astype(jnp.bfloat16))
    own = iota((rows, experts), 0) // capacity == iota((rows, experts), 1) // EXP_NODE
    place = iota((experts, padded), 0) % EXP_NODE + width == iota((experts, padded), 1)
    gates = jnp.dot(
        jnp.where(own, gates, 0.0).astype(jnp.bfloat16), as_bf16(place), preferred_element_type=jnp.float32
    )
    payload_ref[...] = (sent + gates).astype(payload_ref.dtype)


def spread_kernel(capacity, score_ref, shared_ref, out_ref):
    groups = score_ref.shape[0]
    copies, height, lanes = shared_ref.shape
    score = score_ref[...].reshape(groups, score_ref.shape[2])
    held = lanes // capacity
    repeat = as_bf16(iota((capacity, lanes), 0) == iota((capacity, lanes), 1) % capacity)
    own = iota((groups, lanes), 0) % held == iota((groups, lanes), 1) // capacity
    lines = []
    for piece in pieces(score):
        tiled = jnp.where(own, jnp.dot(piece, repeat, preferred_element_type=jnp.float32), 0.0)
        for j in range(groups // held):
            lines.append(jnp.sum(tiled[j * held:(j + 1) * held, :], axis=0, keepdims=True))
    filler = out_ref.shape[1] - height - len(lines)
    lines.append(jnp.zeros((filler, lanes), jnp.float32))
    flat = jnp.concatenate(lines, axis=0).astype(jnp.bfloat16)
    for z in range(copies):
        out_ref[z, :height, :] = shared_ref[z]
        out_ref[z, height:, :] = flat


def router_kernel(capacity, parts_ref, select_ref, ids_ref, scores_ref, out_ref, shared_ref):
    copies, _, lanes = parts_ref.shape
    height = shared_ref.shape[0]
    rows, tokens = select_ref.shape
    lines = rows // lanes
    top = ids_ref.shape[0]
    shares = copies // EXP_NODE
    held = lanes // capacity
    shared = parts_ref[0, :height, :].astype(jnp.float32)
    for z in range(1, copies):
        shared = shared + parts_ref[z, :height, :].astype(jnp.float32)
    shared_ref[...] = shared.astype(shared_ref.dtype)
    ids = ids_ref[...]
    scores = scores_ref[...]
    fold = iota((held, lanes), 0) == iota((held, lanes), 1) // capacity
    score = []
    for c in range(EXP_NODE):
        total = jnp.zeros((lines, lanes), jnp.float32)
        for q in range(shares):
            sent = parts_ref[c * shares + q, height:, :].astype(jnp.float32)
            total = total + (sent[:lines] + sent[lines:2 * lines] + sent[2 * lines:3 * lines])
        score.append(total)
    pick = iota((top, tokens), 0)
    line = iota((EXP_NODE * held, tokens), 0)
    expert = line % held * EXP_NODE + line // held
    contrib = jnp.zeros((top, tokens), jnp.float32)
    for j in range(lines):
        left = jnp.concatenate([jnp.where(fold, score[c][j:j + 1, :], 0.0) for c in range(EXP_NODE)], axis=0)
        found = exact_dot(left, select_ref[j * lanes:(j + 1) * lanes, :])
        for k in range(top):
            mine = jnp.where(expert + j * held * EXP_NODE == ids[k:k + 1, :], found, 0.0)
            contrib = contrib + jnp.where(pick == k, jnp.sum(mine, axis=0, keepdims=True), 0.0)
    totals = jnp.sum(scores, axis=0, keepdims=True)
    mean_term = jnp.sum(scores * contrib, axis=0, keepdims=True) / totals
    out_ref[...] = route_scale / totals * (contrib - mean_term) * scores * (1.0 - scores)


def body(grad_out, expert_ids, gate_scores, saved_hidden, down_weight, shared_weight):
    node_count = lax.axis_size("node")
    local_count = lax.axis_size("local")
    rows_total = saved_hidden.shape[1]
    capacity = rows_total // node_count
    tokens, slice_width = grad_out.shape
    quarter_width = down_weight.shape[0]
    share_count = local_count // EXP_NODE
    padded = (slice_width + EXP_NODE + LANES - 1) // LANES * LANES
    own_expert = lax.axis_index("local") // share_count
    ids = expert_ids.T
    scores = gate_scores.T
    vmem = pl.BlockSpec(memory_space=pltpu.VMEM)
    small = pltpu.CompilerParams(vmem_limit_bytes=KERNEL_VMEM)

    payload, select = pl.pallas_call(
        lambda *refs: route_kernel(capacity, *refs),
        out_shape=(
            jax.ShapeDtypeStruct((rows_total, padded), jnp.bfloat16),
            jax.ShapeDtypeStruct((rows_total, tokens), jnp.bfloat16),
        ),
        in_specs=[vmem] * 3,
        out_specs=(vmem, vmem),
        scratch_shapes=[pltpu.VMEM((padded, tokens), jnp.bfloat16)],
        compiler_params=small,
    )(grad_out.T, ids, scores)
    shared_part = lax.dot_general(
        shared_weight, grad_out, (((1,), (1,)), ((), ())), preferred_element_type=jnp.float32
    ).astype(jnp.bfloat16).reshape(local_count, -1, tokens)
    received = lax.all_to_all(
        payload.reshape(node_count, capacity, padded), "node", split_axis=0, concat_axis=0, tiled=True
    ).reshape(rows_total, padded)

    own_rows = received[:, :slice_width].T
    groups = [list(range(j, local_count, CLASSES)) for j in range(CLASSES)]
    held = lax.all_gather(own_rows, "local", axis=0, tiled=True, axis_index_groups=groups)
    half = held.shape[0] // 2
    lower, upper = held[:half], held[half:]
    right = [(z, (z + 1) % local_count) for z in range(local_count)]
    left = [(z, (z - 1) % local_count) for z in range(local_count)]
    lower_left = lax.ppermute(lower, "local", right)
    upper_right = lax.ppermute(upper, "local", left)
    upper_left = lax.ppermute(upper, "local", right)
    lower_right = lax.ppermute(lower, "local", left)
    lower_far = lax.ppermute(lower_left, "local", right)
    upper_far = lax.ppermute(upper_right, "local", left)

    by_class = down_weight.reshape(quarter_width, 2, -1, CLASSES, slice_width)
    by_class = by_class.transpose(3, 1, 0, 2, 4).reshape(CLASSES, 2, quarter_width, half)

    def partial(rows, shift, part):
        own_class = (lax.axis_index("local") + shift) % CLASSES
        weight = lax.dynamic_index_in_dim(by_class, own_class, 0, keepdims=False)[part]
        return lax.dot_general(rows, weight, (((0,), (1,)), ((), ())), preferred_element_type=jnp.float32)

    hidden_grad = partial(lower, 0, 0) + partial(upper, 0, 1)
    hidden_grad = hidden_grad + partial(lower_left, CLASSES - 1, 0)
    hidden_grad = hidden_grad + partial(upper_right, 1, 1)
    hidden_grad = hidden_grad + partial(upper_left, CLASSES - 1, 1)
    hidden_grad = hidden_grad + partial(lower_right, 1, 0)
    hidden_grad = hidden_grad + partial(lower_far, 2, 0)
    hidden_grad = hidden_grad + partial(upper_far, 2, 1)
    gate_column = lax.dynamic_slice_in_dim(received, slice_width + own_expert, 1, 1).astype(jnp.float32)
    expert_grad = (
        (gate_column * hidden_grad).astype(jnp.bfloat16).reshape(1, rows_total, quarter_width)
    )
    slot_dots = jnp.sum(hidden_grad * saved_hidden[0].astype(jnp.float32), axis=1)

    returned = lax.all_to_all(
        slot_dots.reshape(node_count, 1, capacity), "node", split_axis=0, concat_axis=0, tiled=True
    )
    height = shared_part.shape[1]
    extra = (3 * rows_total // LANES + 15) // 16 * 16
    spread = pl.pallas_call(
        lambda *refs: spread_kernel(capacity, *refs),
        out_shape=jax.ShapeDtypeStruct((local_count, height + extra, tokens), jnp.bfloat16),
        in_specs=[vmem] * 2,
        out_specs=vmem,
        compiler_params=small,
    )(returned, shared_part)
    parts = lax.all_to_all(spread, "local", split_axis=0, concat_axis=0, tiled=True)
    router_grad, shared_grad = pl.pallas_call(
        lambda *refs: router_kernel(capacity, *refs),
        out_shape=(
            jax.ShapeDtypeStruct(scores.shape, jnp.float32),
            jax.ShapeDtypeStruct((height, tokens), jnp.bfloat16),
        ),
        in_specs=[vmem] * 4,
        out_specs=(vmem, vmem),
        compiler_params=small,
    )(parts, select, ids, scores)
    return (expert_grad, router_grad.T, shared_grad)


def solution(mesh):
    return jax.shard_map(
        body,
        mesh=mesh,
        in_specs=(
            P("node", "local"),
            P("node", None),
            P("node", None),
            P("node", None, "local"),
            P(("node", "local"), None),
            P(None, "local"),
        ),
        out_specs=(P("node", None, "local"), P("node", None), P("local", "node")),
        check_vma=False,
    )
```

```python
import jax
import jax.numpy as jnp
from jax import lax
from jax.experimental import pallas as pl
from jax.experimental.pallas import tpu as pltpu
from jax.sharding import PartitionSpec as P

EXP_NODE = 4
LANES = 128
KERNEL_VMEM = 8 << 20

route_scale = 2.5


def iota(shape, dim):
    return lax.broadcasted_iota(jnp.int32, shape, dim)


def as_bf16(mask):
    return mask.astype(jnp.float32).astype(jnp.bfloat16)


def across(left, right):
    return lax.dot_general(left, right, (((1,), (1,)), ((), ())), preferred_element_type=jnp.float32)


def pieces(value):
    high = value.astype(jnp.bfloat16)
    rest = value - high.astype(jnp.float32)
    middle = rest.astype(jnp.bfloat16)
    low = (rest - middle.astype(jnp.float32)).astype(jnp.bfloat16)
    return high, middle, low


def exact_dot(left, right):
    high, middle, low = (jnp.dot(piece, right, preferred_element_type=jnp.float32) for piece in pieces(left))
    return high + middle + low


def route_kernel(capacity, grad_ref, ids_ref, scores_ref, payload_ref, select_ref, wide_ref):
    width, tokens = grad_ref.shape
    rows, padded = payload_ref.shape
    top = ids_ref.shape[0]
    experts = rows // capacity * EXP_NODE
    ids = ids_ref[...]
    scores = scores_ref[...]
    wide_ref[...] = jnp.zeros(wide_ref.shape, wide_ref.dtype)
    wide_ref[:width, :] = grad_ref[...]
    group = iota((rows, tokens), 0) // capacity
    picked = ids // EXP_NODE
    hits = group == picked[0:1, :]
    for k in range(1, top):
        hits = hits | (group == picked[k:k + 1, :])
    hot = hits.astype(jnp.float32)
    before = as_bf16(iota((tokens, tokens), 0) < iota((tokens, tokens), 1))
    rank = jnp.dot(hot.astype(jnp.bfloat16), before, preferred_element_type=jnp.float32)
    slot = (iota((rows, tokens), 0) % capacity).astype(jnp.float32)
    select = jnp.where(rank == slot, hot, 0.0).astype(jnp.bfloat16)
    select_ref[...] = select
    totals = jnp.sum(scores, axis=0, keepdims=True)
    weights = (route_scale * scores / totals).astype(jnp.bfloat16).astype(jnp.float32)
    expert = iota((experts, tokens), 0)
    spread = jnp.zeros((experts, tokens), jnp.float32)
    for k in range(top):
        spread = spread + jnp.where(expert == ids[k:k + 1, :], weights[k:k + 1, :], 0.0)
    sent = across(select, wide_ref[...])
    gates = across(select, spread.astype(jnp.bfloat16))
    own = iota((rows, experts), 0) // capacity == iota((rows, experts), 1) // EXP_NODE
    place = iota((experts, padded), 0) % EXP_NODE + width == iota((experts, padded), 1)
    gates = jnp.dot(
        jnp.where(own, gates, 0.0).astype(jnp.bfloat16), as_bf16(place), preferred_element_type=jnp.float32
    )
    payload_ref[...] = (sent + gates).astype(payload_ref.dtype)


def turn_kernel(received_ref, out_ref):
    width, padded = out_ref.shape[0], received_ref.shape[1]
    keep = as_bf16(iota((width, padded), 0) == iota((width, padded), 1))
    out_ref[...] = across(keep, received_ref[...]).astype(out_ref.dtype)


def spread_kernel(capacity, score_ref, out_ref):
    groups = score_ref.shape[0]
    copies, lines, lanes = out_ref.shape
    score = score_ref[...].reshape(groups, score_ref.shape[2])
    held = lanes // capacity
    repeat = as_bf16(iota((capacity, lanes), 0) == iota((capacity, lanes), 1) % capacity)
    tiled = exact_dot(score, repeat)
    tiled = jnp.where(iota((groups, lanes), 0) % held == iota((groups, lanes), 1) // capacity, tiled, 0.0)
    flat = jnp.concatenate(
        [jnp.sum(tiled[j * held:(j + 1) * held, :], axis=0, keepdims=True) for j in range(lines)], axis=0
    )
    for z in range(copies):
        out_ref[z] = flat


def router_kernel(capacity, parts_ref, select_ref, ids_ref, scores_ref, out_ref):
    copies, lines, lanes = parts_ref.shape
    rows, tokens = select_ref.shape
    top = ids_ref.shape[0]
    shares = copies // EXP_NODE
    held = lanes // capacity
    ids = ids_ref[...]
    scores = scores_ref[...]
    fold = iota((held, lanes), 0) == iota((held, lanes), 1) // capacity
    score = []
    for c in range(EXP_NODE):
        total = parts_ref[c * shares]
        for q in range(1, shares):
            total = total + parts_ref[c * shares + q]
        score.append(total)
    pick = iota((top, tokens), 0)
    line = iota((EXP_NODE * held, tokens), 0)
    expert = line % held * EXP_NODE + line // held
    contrib = jnp.zeros((top, tokens), jnp.float32)
    for j in range(lines):
        left = jnp.concatenate([jnp.where(fold, score[c][j:j + 1, :], 0.0) for c in range(EXP_NODE)], axis=0)
        found = exact_dot(left, select_ref[j * lanes:(j + 1) * lanes, :])
        for k in range(top):
            mine = jnp.where(expert + j * held * EXP_NODE == ids[k:k + 1, :], found, 0.0)
            contrib = contrib + jnp.where(pick == k, jnp.sum(mine, axis=0, keepdims=True), 0.0)
    totals = jnp.sum(scores, axis=0, keepdims=True)
    mean_term = jnp.sum(scores * contrib, axis=0, keepdims=True) / totals
    out_ref[...] = route_scale / totals * (contrib - mean_term) * scores * (1.0 - scores)


def ring_sum(part, count):
    me = lax.axis_index("local")
    right = [(z, (z + 1) % count) for z in range(count)]
    left = [(z, (z - 1) % count) for z in range(count)]

    def block(offset):
        return lax.dynamic_index_in_dim(part, lax.rem(me + (offset + count), count), 0, keepdims=False)

    def send(running, links):
        return lax.ppermute(running.astype(jnp.bfloat16), "local", links).astype(jnp.float32)

    ahead, behind = count // 2, (count - 1) // 2
    from_left = send(block(ahead), right)
    from_right = send(block(-behind), left)
    for step in range(1, ahead):
        from_left = send(from_left + block(ahead - step), right)
        if step < behind:
            from_right = send(from_right + block(step - behind), left)
    return (from_left + from_right + block(0)).astype(jnp.bfloat16)


def body(grad_out, expert_ids, gate_scores, saved_hidden, down_weight, shared_weight):
    node_count = lax.axis_size("node")
    local_count = lax.axis_size("local")
    rows_total = saved_hidden.shape[1]
    capacity = rows_total // node_count
    tokens, slice_width = grad_out.shape
    quarter_width = down_weight.shape[0]
    share_count = local_count // EXP_NODE
    padded = (slice_width + EXP_NODE + LANES - 1) // LANES * LANES
    own_expert = lax.axis_index("local") // share_count
    ids = expert_ids.T
    scores = gate_scores.T
    vmem = pl.BlockSpec(memory_space=pltpu.VMEM)
    small = pltpu.CompilerParams(vmem_limit_bytes=KERNEL_VMEM)

    payload, select = pl.pallas_call(
        lambda *refs: route_kernel(capacity, *refs),
        out_shape=(
            jax.ShapeDtypeStruct((rows_total, padded), jnp.bfloat16),
            jax.ShapeDtypeStruct((rows_total, tokens), jnp.bfloat16),
        ),
        in_specs=[vmem] * 3,
        out_specs=(vmem, vmem),
        scratch_shapes=[pltpu.VMEM((padded, tokens), jnp.bfloat16)],
        compiler_params=small,
    )(grad_out.T, ids, scores)
    shared_part = lax.dot_general(
        shared_weight, grad_out, (((1,), (1,)), ((), ())), preferred_element_type=jnp.float32
    ).reshape(local_count, -1, tokens)
    received = lax.all_to_all(
        payload.reshape(node_count, capacity, padded), "node", split_axis=0, concat_axis=0, tiled=True
    ).reshape(rows_total, padded)

    own_rows = pl.pallas_call(
        turn_kernel,
        out_shape=jax.ShapeDtypeStruct((slice_width, rows_total), jnp.bfloat16),
        in_specs=[vmem],
        out_specs=vmem,
        compiler_params=small,
    )(received)
    full_rows = lax.all_gather(own_rows, "local", axis=0, tiled=True)

    shared_part, _ = lax.optimization_barrier((shared_part, own_rows))
    shared_grad = ring_sum(shared_part, local_count)
    full_rows, shared_grad = lax.optimization_barrier((full_rows, shared_grad))

    hidden_grad = lax.dot_general(
        full_rows, down_weight, (((0,), (1,)), ((), ())), preferred_element_type=jnp.float32
    )
    gate_column = lax.dynamic_slice_in_dim(received, slice_width + own_expert, 1, 1).astype(jnp.float32)
    expert_grad = (
        (gate_column * hidden_grad).astype(jnp.bfloat16).reshape(1, rows_total, quarter_width)
    )
    slot_dots = jnp.sum(hidden_grad * saved_hidden[0].astype(jnp.float32), axis=1)

    returned = lax.all_to_all(
        slot_dots.reshape(node_count, 1, capacity), "node", split_axis=0, concat_axis=0, tiled=True
    )
    spread = pl.pallas_call(
        lambda *refs: spread_kernel(capacity, *refs),
        out_shape=jax.ShapeDtypeStruct((local_count, rows_total // LANES, LANES), jnp.float32),
        in_specs=[vmem],
        out_specs=vmem,
        compiler_params=small,
    )(returned)
    parts = lax.all_to_all(spread, "local", split_axis=0, concat_axis=0, tiled=True)
    router_grad = pl.pallas_call(
        lambda *refs: router_kernel(capacity, *refs),
        out_shape=jax.ShapeDtypeStruct(scores.shape, jnp.float32),
        in_specs=[vmem] * 4,
        out_specs=vmem,
        compiler_params=small,
    )(parts, select, ids, scores)
    return (expert_grad, router_grad.T, shared_grad)


def solution(mesh):
    return jax.shard_map(
        body,
        mesh=mesh,
        in_specs=(
            P("node", "local"),
            P("node", None),
            P("node", None),
            P("node", None, "local"),
            P(("node", "local"), None),
            P(None, "local"),
        ),
        out_specs=(P("node", None, "local"), P("node", None), P("local", "node")),
        check_vma=False,
    )
```

```python
import jax
import jax.numpy as jnp
from jax import lax
from jax.experimental import pallas as pl
from jax.experimental.pallas import tpu as pltpu
from jax.sharding import PartitionSpec as P

EXP_NODE = 4
LANES = 128
KERNEL_VMEM = 8 << 20

route_scale = 2.5


def iota(shape, dim):
    return lax.broadcasted_iota(jnp.int32, shape, dim)


def as_bf16(mask):
    return mask.astype(jnp.float32).astype(jnp.bfloat16)


def across(left, right):
    return lax.dot_general(left, right, (((1,), (1,)), ((), ())), preferred_element_type=jnp.float32)


def pieces(value):
    high = value.astype(jnp.bfloat16)
    rest = value - high.astype(jnp.float32)
    middle = rest.astype(jnp.bfloat16)
    low = (rest - middle.astype(jnp.float32)).astype(jnp.bfloat16)
    return high, middle, low


def exact_dot(left, right):
    high, middle, low = (jnp.dot(piece, right, preferred_element_type=jnp.float32) for piece in pieces(left))
    return high + middle + low


def route_kernel(capacity, grad_ref, ids_ref, scores_ref, payload_ref, select_ref, wide_ref):
    width, tokens = grad_ref.shape
    rows, padded = payload_ref.shape
    top = ids_ref.shape[0]
    experts = rows // capacity * EXP_NODE
    ids = ids_ref[...]
    scores = scores_ref[...]
    wide_ref[...] = jnp.zeros(wide_ref.shape, wide_ref.dtype)
    wide_ref[:width, :] = grad_ref[...]
    group = iota((rows, tokens), 0) // capacity
    picked = ids // EXP_NODE
    hits = group == picked[0:1, :]
    for k in range(1, top):
        hits = hits | (group == picked[k:k + 1, :])
    hot = hits.astype(jnp.float32)
    before = as_bf16(iota((tokens, tokens), 0) < iota((tokens, tokens), 1))
    rank = jnp.dot(hot.astype(jnp.bfloat16), before, preferred_element_type=jnp.float32)
    slot = (iota((rows, tokens), 0) % capacity).astype(jnp.float32)
    select = jnp.where(rank == slot, hot, 0.0).astype(jnp.bfloat16)
    select_ref[...] = select
    totals = jnp.sum(scores, axis=0, keepdims=True)
    weights = (route_scale * scores / totals).astype(jnp.bfloat16).astype(jnp.float32)
    expert = iota((experts, tokens), 0)
    spread = jnp.zeros((experts, tokens), jnp.float32)
    for k in range(top):
        spread = spread + jnp.where(expert == ids[k:k + 1, :], weights[k:k + 1, :], 0.0)
    sent = across(select, wide_ref[...])
    gates = across(select, spread.astype(jnp.bfloat16))
    own = iota((rows, experts), 0) // capacity == iota((rows, experts), 1) // EXP_NODE
    place = iota((experts, padded), 0) % EXP_NODE + width == iota((experts, padded), 1)
    gates = jnp.dot(
        jnp.where(own, gates, 0.0).astype(jnp.bfloat16), as_bf16(place), preferred_element_type=jnp.float32
    )
    payload_ref[...] = (sent + gates).astype(payload_ref.dtype)


def turn_kernel(received_ref, out_ref):
    width, padded = out_ref.shape[0], received_ref.shape[1]
    keep = as_bf16(iota((width, padded), 0) == iota((width, padded), 1))
    out_ref[...] = across(keep, received_ref[...]).astype(out_ref.dtype)


def spread_kernel(capacity, score_ref, out_ref):
    groups = score_ref.shape[0]
    copies, lines, lanes = out_ref.shape
    score = score_ref[...].reshape(groups, score_ref.shape[2])
    held = lanes // capacity
    repeat = as_bf16(iota((capacity, lanes), 0) == iota((capacity, lanes), 1) % capacity)
    tiled = exact_dot(score, repeat)
    tiled = jnp.where(iota((groups, lanes), 0) % held == iota((groups, lanes), 1) // capacity, tiled, 0.0)
    flat = jnp.concatenate(
        [jnp.sum(tiled[j * held:(j + 1) * held, :], axis=0, keepdims=True) for j in range(lines)], axis=0
    )
    for z in range(copies):
        out_ref[z] = flat


def router_kernel(capacity, parts_ref, select_ref, ids_ref, scores_ref, out_ref):
    copies, lines, lanes = parts_ref.shape
    rows, tokens = select_ref.shape
    top = ids_ref.shape[0]
    shares = copies // EXP_NODE
    held = lanes // capacity
    ids = ids_ref[...]
    scores = scores_ref[...]
    fold = iota((held, lanes), 0) == iota((held, lanes), 1) // capacity
    score = []
    for c in range(EXP_NODE):
        total = parts_ref[c * shares]
        for q in range(1, shares):
            total = total + parts_ref[c * shares + q]
        score.append(total)
    pick = iota((top, tokens), 0)
    line = iota((EXP_NODE * held, tokens), 0)
    expert = line % held * EXP_NODE + line // held
    contrib = jnp.zeros((top, tokens), jnp.float32)
    for j in range(lines):
        left = jnp.concatenate([jnp.where(fold, score[c][j:j + 1, :], 0.0) for c in range(EXP_NODE)], axis=0)
        found = exact_dot(left, select_ref[j * lanes:(j + 1) * lanes, :])
        for k in range(top):
            mine = jnp.where(expert + j * held * EXP_NODE == ids[k:k + 1, :], found, 0.0)
            contrib = contrib + jnp.where(pick == k, jnp.sum(mine, axis=0, keepdims=True), 0.0)
    totals = jnp.sum(scores, axis=0, keepdims=True)
    mean_term = jnp.sum(scores * contrib, axis=0, keepdims=True) / totals
    out_ref[...] = route_scale / totals * (contrib - mean_term) * scores * (1.0 - scores)


def ring_sum(part, count):
    me = lax.axis_index("local")
    parity, place, half = me % 2, me // 2, count // 2
    swap = [(z, z ^ 1) for z in range(count)]
    right = [(z, (z + 2) % count) for z in range(count)]
    left = [(z, (z - 2) % count) for z in range(count)]

    def send(running, links):
        return lax.ppermute(running.astype(jnp.bfloat16), "local", links).astype(jnp.float32)

    pairs = part.reshape((half, 2) + part.shape[1:])
    given = lax.dynamic_index_in_dim(pairs, 1 - parity, 1, keepdims=False)
    kept = lax.dynamic_index_in_dim(pairs, parity, 1, keepdims=False) + send(given, swap)

    def block(offset):
        return lax.dynamic_index_in_dim(kept, lax.rem(place + (offset + half), half), 0, keepdims=False)

    ahead, behind = half // 2, (half - 1) // 2
    from_left = send(block(ahead), right)
    from_right = send(block(-behind), left)
    for step in range(1, ahead):
        from_left = send(from_left + block(ahead - step), right)
        if step < behind:
            from_right = send(from_right + block(step - behind), left)
    return (from_left + from_right + block(0)).astype(jnp.bfloat16)


def body(grad_out, expert_ids, gate_scores, saved_hidden, down_weight, shared_weight):
    node_count = lax.axis_size("node")
    local_count = lax.axis_size("local")
    rows_total = saved_hidden.shape[1]
    capacity = rows_total // node_count
    tokens, slice_width = grad_out.shape
    quarter_width = down_weight.shape[0]
    share_count = local_count // EXP_NODE
    padded = (slice_width + EXP_NODE + LANES - 1) // LANES * LANES
    own_expert = lax.axis_index("local") // share_count
    ids = expert_ids.T
    scores = gate_scores.T
    vmem = pl.BlockSpec(memory_space=pltpu.VMEM)
    small = pltpu.CompilerParams(vmem_limit_bytes=KERNEL_VMEM)

    payload, select = pl.pallas_call(
        lambda *refs: route_kernel(capacity, *refs),
        out_shape=(
            jax.ShapeDtypeStruct((rows_total, padded), jnp.bfloat16),
            jax.ShapeDtypeStruct((rows_total, tokens), jnp.bfloat16),
        ),
        scratch_shapes=[pltpu.VMEM((padded, tokens), jnp.bfloat16)],
    )(grad_out.T, ids, scores)
    shared_part = lax.dot_general(
        shared_weight, grad_out, (((1,), (1,)), ((), ())), preferred_element_type=jnp.float32
    ).reshape(local_count, -1, tokens)
    received = lax.all_to_all(
        payload.reshape(node_count, capacity, padded), "node", split_axis=0, concat_axis=0, tiled=True
    ).reshape(rows_total, padded)

    own_rows = pl.pallas_call(
        turn_kernel,
        out_shape=jax.ShapeDtypeStruct((slice_width, rows_total), jnp.bfloat16),
        in_specs=[vmem],
        out_specs=vmem,
        compiler_params=small,
    )(received)
    full_rows = lax.all_gather(own_rows, "local", axis=0, tiled=True)

    shared_part, _ = lax.optimization_barrier((shared_part, own_rows))
    shared_grad = ring_sum(shared_part, local_count)
    full_rows, shared_grad = lax.optimization_barrier((full_rows, shared_grad))

    hidden_grad = lax.dot_general(
        full_rows, down_weight, (((0,), (1,)), ((), ())), preferred_element_type=jnp.float32
    )
    gate_column = lax.dynamic_slice_in_dim(received, slice_width + own_expert, 1, 1).astype(jnp.float32)
    expert_grad = (
        (gate_column * hidden_grad).astype(jnp.bfloat16).reshape(1, rows_total, quarter_width)
    )
    slot_dots = jnp.sum(hidden_grad * saved_hidden[0].astype(jnp.float32), axis=1)

    returned = lax.all_to_all(
        slot_dots.reshape(node_count, 1, capacity), "node", split_axis=0, concat_axis=0, tiled=True
    )
    spread = pl.pallas_call(
        lambda *refs: spread_kernel(capacity, *refs),
        out_shape=jax.ShapeDtypeStruct((local_count, rows_total // LANES, LANES), jnp.float32),
        in_specs=[vmem],
        out_specs=vmem,
        compiler_params=small,
    )(returned)
    parts = lax.all_to_all(spread, "local", split_axis=0, concat_axis=0, tiled=True)
    router_grad = pl.pallas_call(
        lambda *refs: router_kernel(capacity, *refs),
        out_shape=jax.ShapeDtypeStruct(scores.shape, jnp.float32),
        in_specs=[vmem] * 4,
        out_specs=vmem,
        compiler_params=small,
    )(parts, select, ids, scores)
    return (expert_grad, router_grad.T, shared_grad)


def solution(mesh):
    return jax.shard_map(
        body,
        mesh=mesh,
        in_specs=(
            P("node", "local"),
            P("node", None),
            P("node", None),
            P("node", None, "local"),
            P(("node", "local"), None),
            P(None, "local"),
        ),
        out_specs=(P("node", None, "local"), P("node", None), P("local", "node")),
        check_vma=False,
    )
```

```python
import jax
import jax.numpy as jnp
from jax import lax
from jax.experimental import pallas as pl
from jax.experimental.pallas import tpu as pltpu
from jax.sharding import PartitionSpec as P

EXP_NODE = 4
LANES = 128
CLASSES = 4
KERNEL_VMEM = 8 << 20

route_scale = 2.5


def iota(shape, dim):
    return lax.broadcasted_iota(jnp.int32, shape, dim)


def as_bf16(mask):
    return mask.astype(jnp.float32).astype(jnp.bfloat16)


def across(left, right):
    return lax.dot_general(left, right, (((1,), (1,)), ((), ())), preferred_element_type=jnp.float32)


def pieces(value):
    high = value.astype(jnp.bfloat16)
    rest = value - high.astype(jnp.float32)
    middle = rest.astype(jnp.bfloat16)
    low = (rest - middle.astype(jnp.float32)).astype(jnp.bfloat16)
    return high, middle, low


def exact_dot(left, right):
    high, middle, low = (jnp.dot(piece, right, preferred_element_type=jnp.float32) for piece in pieces(left))
    return high + middle + low


def route_kernel(capacity, grad_ref, ids_ref, scores_ref, payload_ref, select_ref, wide_ref):
    width, tokens = grad_ref.shape
    rows, padded = payload_ref.shape
    top = ids_ref.shape[0]
    experts = rows // capacity * EXP_NODE
    ids = ids_ref[...]
    scores = scores_ref[...]
    wide_ref[...] = jnp.zeros(wide_ref.shape, wide_ref.dtype)
    wide_ref[:width, :] = grad_ref[...]
    group = iota((rows, tokens), 0) // capacity
    picked = ids // EXP_NODE
    hits = group == picked[0:1, :]
    for k in range(1, top):
        hits = hits | (group == picked[k:k + 1, :])
    hot = hits.astype(jnp.float32)
    before = as_bf16(iota((tokens, tokens), 0) < iota((tokens, tokens), 1))
    rank = jnp.dot(hot.astype(jnp.bfloat16), before, preferred_element_type=jnp.float32)
    slot = (iota((rows, tokens), 0) % capacity).astype(jnp.float32)
    select = jnp.where(rank == slot, hot, 0.0).astype(jnp.bfloat16)
    select_ref[...] = select
    totals = jnp.sum(scores, axis=0, keepdims=True)
    weights = (route_scale * scores / totals).astype(jnp.bfloat16).astype(jnp.float32)
    expert = iota((experts, tokens), 0)
    spread = jnp.zeros((experts, tokens), jnp.float32)
    for k in range(top):
        spread = spread + jnp.where(expert == ids[k:k + 1, :], weights[k:k + 1, :], 0.0)
    sent = across(select, wide_ref[...])
    gates = across(select, spread.astype(jnp.bfloat16))
    own = iota((rows, experts), 0) // capacity == iota((rows, experts), 1) // EXP_NODE
    place = iota((experts, padded), 0) % EXP_NODE + width == iota((experts, padded), 1)
    gates = jnp.dot(
        jnp.where(own, gates, 0.0).astype(jnp.bfloat16), as_bf16(place), preferred_element_type=jnp.float32
    )
    payload_ref[...] = (sent + gates).astype(payload_ref.dtype)


def turn_kernel(received_ref, out_ref):
    width, padded = out_ref.shape[0], received_ref.shape[1]
    keep = as_bf16(iota((width, padded), 0) == iota((width, padded), 1))
    out_ref[...] = across(keep, received_ref[...]).astype(out_ref.dtype)


def spread_kernel(capacity, score_ref, shared_ref, out_ref):
    groups = score_ref.shape[0]
    copies, height, lanes = shared_ref.shape
    score = score_ref[...].reshape(groups, score_ref.shape[2])
    held = lanes // capacity
    repeat = as_bf16(iota((capacity, lanes), 0) == iota((capacity, lanes), 1) % capacity)
    own = iota((groups, lanes), 0) % held == iota((groups, lanes), 1) // capacity
    lines = []
    for piece in pieces(score):
        tiled = jnp.where(own, jnp.dot(piece, repeat, preferred_element_type=jnp.float32), 0.0)
        for j in range(groups // held):
            lines.append(jnp.sum(tiled[j * held:(j + 1) * held, :], axis=0, keepdims=True))
    filler = out_ref.shape[1] - height - len(lines)
    lines.append(jnp.zeros((filler, lanes), jnp.float32))
    flat = jnp.concatenate(lines, axis=0).astype(jnp.bfloat16)
    for z in range(copies):
        out_ref[z, :height, :] = shared_ref[z]
        out_ref[z, height:, :] = flat


def router_kernel(capacity, parts_ref, select_ref, ids_ref, scores_ref, out_ref, shared_ref):
    copies, _, lanes = parts_ref.shape
    height = shared_ref.shape[0] // 2
    rows, tokens = select_ref.shape
    lines = rows // lanes
    top = ids_ref.shape[0]
    shares = copies // EXP_NODE
    held = lanes // capacity
    for parity in range(2):
        shared = parts_ref[parity, :height, :].astype(jnp.float32)
        for z in range(parity + 2, copies, 2):
            shared = shared + parts_ref[z, :height, :].astype(jnp.float32)
        shared_ref[parity * height:(parity + 1) * height, :] = shared.astype(shared_ref.dtype)
    ids = ids_ref[...]
    scores = scores_ref[...]
    fold = iota((held, lanes), 0) == iota((held, lanes), 1) // capacity
    score = []
    for c in range(EXP_NODE):
        total = jnp.zeros((lines, lanes), jnp.float32)
        for q in range(shares):
            sent = parts_ref[c * shares + q, height:, :].astype(jnp.float32)
            total = total + (sent[:lines] + sent[lines:2 * lines] + sent[2 * lines:3 * lines])
        score.append(total)
    pick = iota((top, tokens), 0)
    line = iota((EXP_NODE * held, tokens), 0)
    expert = line % held * EXP_NODE + line // held
    contrib = jnp.zeros((top, tokens), jnp.float32)
    for j in range(lines):
        left = jnp.concatenate([jnp.where(fold, score[c][j:j + 1, :], 0.0) for c in range(EXP_NODE)], axis=0)
        found = exact_dot(left, select_ref[j * lanes:(j + 1) * lanes, :])
        for k in range(top):
            mine = jnp.where(expert + j * held * EXP_NODE == ids[k:k + 1, :], found, 0.0)
            contrib = contrib + jnp.where(pick == k, jnp.sum(mine, axis=0, keepdims=True), 0.0)
    totals = jnp.sum(scores, axis=0, keepdims=True)
    mean_term = jnp.sum(scores * contrib, axis=0, keepdims=True) / totals
    out_ref[...] = route_scale / totals * (contrib - mean_term) * scores * (1.0 - scores)


def swap_halves(part, count):
    parity = lax.axis_index("local") % 2
    given = lax.dynamic_index_in_dim(part, 1 - parity, 1, keepdims=False).astype(jnp.bfloat16)
    swapped = lax.ppermute(given, "local", [(z, z ^ 1) for z in range(count)])
    kept = lax.dynamic_index_in_dim(part, parity, 1, keepdims=False)
    return (kept + swapped.astype(jnp.float32)).astype(jnp.bfloat16)


def body(grad_out, expert_ids, gate_scores, saved_hidden, down_weight, shared_weight):
    node_count = lax.axis_size("node")
    local_count = lax.axis_size("local")
    rows_total = saved_hidden.shape[1]
    capacity = rows_total // node_count
    tokens, slice_width = grad_out.shape
    quarter_width = down_weight.shape[0]
    share_count = local_count // EXP_NODE
    padded = (slice_width + EXP_NODE + LANES - 1) // LANES * LANES
    own_expert = lax.axis_index("local") // share_count
    ids = expert_ids.T
    scores = gate_scores.T
    vmem = pl.BlockSpec(memory_space=pltpu.VMEM)
    small = pltpu.CompilerParams(vmem_limit_bytes=KERNEL_VMEM)

    payload, select = pl.pallas_call(
        lambda *refs: route_kernel(capacity, *refs),
        out_shape=(
            jax.ShapeDtypeStruct((rows_total, padded), jnp.bfloat16),
            jax.ShapeDtypeStruct((rows_total, tokens), jnp.bfloat16),
        ),
        scratch_shapes=[pltpu.VMEM((padded, tokens), jnp.bfloat16)],
    )(grad_out.T, ids, scores)
    payload, grad_late = lax.optimization_barrier((payload, grad_out))
    shared_part = lax.dot_general(
        shared_weight, grad_late, (((1,), (1,)), ((), ())), preferred_element_type=jnp.float32
    )
    shared_part = swap_halves(shared_part.reshape(local_count, 2, -1, tokens), local_count)
    received = lax.all_to_all(
        payload.reshape(node_count, capacity, padded), "node", split_axis=0, concat_axis=0, tiled=True
    ).reshape(rows_total, padded)
    received, shared_part = lax.optimization_barrier((received, shared_part))

    own_rows = pl.pallas_call(
        turn_kernel,
        out_shape=jax.ShapeDtypeStruct((slice_width, rows_total), jnp.bfloat16),
        in_specs=[vmem],
        out_specs=vmem,
        compiler_params=small,
    )(received)
    groups = [list(range(j, local_count, CLASSES)) for j in range(CLASSES)]
    held = lax.all_gather(own_rows, "local", axis=0, tiled=True, axis_index_groups=groups)
    half = held.shape[0] // 2
    lower, upper = held[:half], held[half:]
    right = [(z, (z + 1) % local_count) for z in range(local_count)]
    left = [(z, (z - 1) % local_count) for z in range(local_count)]
    by_class = down_weight.reshape(quarter_width, 2, -1, CLASSES, slice_width)
    by_class = by_class.transpose(3, 1, 0, 2, 4).reshape(CLASSES, 2, quarter_width, half)

    def partial(rows, shift, part):
        own_class = (lax.axis_index("local") + shift) % CLASSES
        weight = lax.dynamic_index_in_dim(by_class, own_class, 0, keepdims=False)[part]
        return lax.dot_general(rows, weight, (((0,), (1,)), ((), ())), preferred_element_type=jnp.float32)

    lower_left = lax.ppermute(lower, "local", right)
    upper_right = lax.ppermute(upper, "local", left)
    hidden_grad = partial(lower, 0, 0) + partial(upper, 0, 1)
    lower, upper, hidden_grad = lax.optimization_barrier((lower, upper, hidden_grad))
    upper_left = lax.ppermute(upper, "local", right)
    lower_right = lax.ppermute(lower, "local", left)
    lower_far = lax.ppermute(lower_left, "local", right)
    upper_far = lax.ppermute(upper_right, "local", left)
    hidden_grad = hidden_grad + partial(lower_left, CLASSES - 1, 0)
    hidden_grad = hidden_grad + partial(upper_right, 1, 1)
    hidden_grad = hidden_grad + partial(upper_left, CLASSES - 1, 1)
    hidden_grad = hidden_grad + partial(lower_right, 1, 0)
    hidden_grad = hidden_grad + partial(lower_far, 2, 0)
    hidden_grad = hidden_grad + partial(upper_far, 2, 1)
    gate_column = lax.dynamic_slice_in_dim(received, slice_width + own_expert, 1, 1).astype(jnp.float32)
    expert_grad = (
        (gate_column * hidden_grad).astype(jnp.bfloat16).reshape(1, rows_total, quarter_width)
    )
    slot_dots = jnp.sum(hidden_grad * saved_hidden[0].astype(jnp.float32), axis=1)

    returned = lax.all_to_all(
        slot_dots.reshape(node_count, 1, capacity), "node", split_axis=0, concat_axis=0, tiled=True
    )
    height = shared_part.shape[1]
    extra = (3 * rows_total // LANES + 15) // 16 * 16
    spread = pl.pallas_call(
        lambda *refs: spread_kernel(capacity, *refs),
        out_shape=jax.ShapeDtypeStruct((local_count, height + extra, tokens), jnp.bfloat16),
        in_specs=[vmem] * 2,
        out_specs=vmem,
        compiler_params=small,
    )(returned, shared_part)
    parts = lax.all_to_all(spread, "local", split_axis=0, concat_axis=0, tiled=True)
    router_grad, shared_grad = pl.pallas_call(
        lambda *refs: router_kernel(capacity, *refs),
        out_shape=(
            jax.ShapeDtypeStruct(scores.shape, jnp.float32),
            jax.ShapeDtypeStruct((2 * height, tokens), jnp.bfloat16),
        ),
        in_specs=[vmem] * 4,
        out_specs=(vmem, vmem),
        compiler_params=small,
    )(parts, select, ids, scores)
    return (expert_grad, router_grad.T, shared_grad)


def solution(mesh):
    return jax.shard_map(
        body,
        mesh=mesh,
        in_specs=(
            P("node", "local"),
            P("node", None),
            P("node", None),
            P("node", None, "local"),
            P(("node", "local"), None),
            P(None, "local"),
        ),
        out_specs=(P("node", None, "local"), P("node", None), P("local", "node")),
        check_vma=False,
    )
```

```python
import jax
import jax.numpy as jnp
from jax import lax
from jax.experimental import pallas as pl
from jax.experimental.pallas import tpu as pltpu
from jax.sharding import PartitionSpec as P

EXP_NODE = 4
LANES = 128
CLASSES = 4
KERNEL_VMEM = 8 << 20

route_scale = 2.5


def iota(shape, dim):
    return lax.broadcasted_iota(jnp.int32, shape, dim)


def as_bf16(mask):
    return mask.astype(jnp.float32).astype(jnp.bfloat16)


def across(left, right):
    return lax.dot_general(left, right, (((1,), (1,)), ((), ())), preferred_element_type=jnp.float32)


def pieces(value):
    high = value.astype(jnp.bfloat16)
    rest = value - high.astype(jnp.float32)
    middle = rest.astype(jnp.bfloat16)
    low = (rest - middle.astype(jnp.float32)).astype(jnp.bfloat16)
    return high, middle, low


def exact_dot(left, right):
    high, middle, low = (jnp.dot(piece, right, preferred_element_type=jnp.float32) for piece in pieces(left))
    return high + middle + low


def route_kernel(capacity, grad_ref, ids_ref, scores_ref, payload_ref, select_ref):
    width, tokens = grad_ref.shape
    rows, padded = payload_ref.shape
    top = ids_ref.shape[0]
    experts = rows // capacity * EXP_NODE
    ids = ids_ref[...]
    scores = scores_ref[...]
    group = iota((rows, tokens), 0) // capacity
    picked = ids // EXP_NODE
    hits = group == picked[0:1, :]
    for k in range(1, top):
        hits = hits | (group == picked[k:k + 1, :])
    hot = hits.astype(jnp.float32)
    before = as_bf16(iota((tokens, tokens), 0) < iota((tokens, tokens), 1))
    rank = jnp.dot(hot.astype(jnp.bfloat16), before, preferred_element_type=jnp.float32)
    slot = (iota((rows, tokens), 0) % capacity).astype(jnp.float32)
    select = jnp.where(rank == slot, hot, 0.0).astype(jnp.bfloat16)
    select_ref[...] = select
    totals = jnp.sum(scores, axis=0, keepdims=True)
    weights = (route_scale * scores / totals).astype(jnp.bfloat16).astype(jnp.float32)
    expert = iota((experts, tokens), 0)
    spread = jnp.zeros((experts, tokens), jnp.float32)
    for k in range(top):
        spread = spread + jnp.where(expert == ids[k:k + 1, :], weights[k:k + 1, :], 0.0)
    payload_ref[:, :width] = across(select, grad_ref[...]).astype(payload_ref.dtype)
    gates = across(select, spread.astype(jnp.bfloat16))
    own = iota((rows, experts), 0) // capacity == iota((rows, experts), 1) // EXP_NODE
    place = iota((experts, padded - width), 0) % EXP_NODE == iota((experts, padded - width), 1)
    gates = jnp.dot(
        jnp.where(own, gates, 0.0).astype(jnp.bfloat16), as_bf16(place), preferred_element_type=jnp.float32
    )
    payload_ref[:, width:] = gates.astype(payload_ref.dtype)


def spread_kernel(capacity, score_ref, shared_ref, out_ref):
    groups = score_ref.shape[0]
    copies, height, lanes = shared_ref.shape
    score = score_ref[...].reshape(groups, score_ref.shape[2])
    held = lanes // capacity
    repeat = as_bf16(iota((capacity, lanes), 0) == iota((capacity, lanes), 1) % capacity)
    own = iota((groups, lanes), 0) % held == iota((groups, lanes), 1) // capacity
    lines = []
    for piece in pieces(score):
        tiled = jnp.where(own, jnp.dot(piece, repeat, preferred_element_type=jnp.float32), 0.0)
        for j in range(groups // held):
            lines.append(jnp.sum(tiled[j * held:(j + 1) * held, :], axis=0, keepdims=True))
    filler = out_ref.shape[1] - height - len(lines)
    lines.append(jnp.zeros((filler, lanes), jnp.float32))
    flat = jnp.concatenate(lines, axis=0).astype(jnp.bfloat16)
    for z in range(copies):
        out_ref[z, :height, :] = shared_ref[z]
        out_ref[z, height:, :] = flat


def router_kernel(capacity, parts_ref, select_ref, ids_ref, scores_ref, out_ref, shared_ref):
    copies, _, lanes = parts_ref.shape
    height = shared_ref.shape[0] // 4
    rows, tokens = select_ref.shape
    lines = rows // lanes
    top = ids_ref.shape[0]
    shares = copies // EXP_NODE
    held = lanes // capacity
    for first in range(4):
        shared = parts_ref[first, :height, :].astype(jnp.float32)
        for z in range(first + 4, copies, 4):
            shared = shared + parts_ref[z, :height, :].astype(jnp.float32)
        start = (first % 2 * 2 + first // 2) * height
        shared_ref[start:start + height, :] = shared.astype(shared_ref.dtype)
    ids = ids_ref[...]
    scores = scores_ref[...]
    fold = iota((held, lanes), 0) == iota((held, lanes), 1) // capacity
    score = []
    for c in range(EXP_NODE):
        total = jnp.zeros((lines, lanes), jnp.float32)
        for q in range(shares):
            sent = parts_ref[c * shares + q, height:, :].astype(jnp.float32)
            total = total + (sent[:lines] + sent[lines:2 * lines] + sent[2 * lines:3 * lines])
        score.append(total)
    pick = iota((top, tokens), 0)
    line = iota((EXP_NODE * held, tokens), 0)
    expert = line % held * EXP_NODE + line // held
    contrib = jnp.zeros((top, tokens), jnp.float32)
    for j in range(lines):
        left = jnp.concatenate([jnp.where(fold, score[c][j:j + 1, :], 0.0) for c in range(EXP_NODE)], axis=0)
        found = exact_dot(left, select_ref[j * lanes:(j + 1) * lanes, :])
        for k in range(top):
            mine = jnp.where(expert + j * held * EXP_NODE == ids[k:k + 1, :], found, 0.0)
            contrib = contrib + jnp.where(pick == k, jnp.sum(mine, axis=0, keepdims=True), 0.0)
    totals = jnp.sum(scores, axis=0, keepdims=True)
    mean_term = jnp.sum(scores * contrib, axis=0, keepdims=True) / totals
    out_ref[...] = route_scale / totals * (contrib - mean_term) * scores * (1.0 - scores)


def swap_halves(part, count, bit):
    kept = lax.axis_index("local") // bit % 2
    halves = part.reshape(count, 2, -1, part.shape[2])
    given = lax.dynamic_index_in_dim(halves, 1 - kept, 1, keepdims=False).astype(jnp.bfloat16)
    swapped = lax.ppermute(given, "local", [(z, z ^ bit) for z in range(count)])
    return lax.dynamic_index_in_dim(halves, kept, 1, keepdims=False) + swapped.astype(jnp.float32)


def body(grad_out, expert_ids, gate_scores, saved_hidden, down_weight, shared_weight):
    node_count = lax.axis_size("node")
    local_count = lax.axis_size("local")
    rows_total = saved_hidden.shape[1]
    capacity = rows_total // node_count
    tokens, slice_width = grad_out.shape
    quarter_width = down_weight.shape[0]
    share_count = local_count // EXP_NODE
    class_width = slice_width * local_count // CLASSES
    padded = class_width + LANES
    own_expert = lax.axis_index("local") // share_count
    ids = expert_ids.T
    scores = gate_scores.T
    vmem = pl.BlockSpec(memory_space=pltpu.VMEM)
    small = pltpu.CompilerParams(vmem_limit_bytes=KERNEL_VMEM)

    groups = [list(range(j, local_count, CLASSES)) for j in range(CLASSES)]
    class_grad = lax.all_gather(grad_out.T, "local", axis=0, tiled=True, axis_index_groups=groups)
    payload, select = pl.pallas_call(
        lambda *refs: route_kernel(capacity, *refs),
        out_shape=(
            jax.ShapeDtypeStruct((rows_total, padded), jnp.bfloat16),
            jax.ShapeDtypeStruct((rows_total, tokens), jnp.bfloat16),
        ),
        compiler_params=pltpu.CompilerParams(vmem_limit_bytes=2 * KERNEL_VMEM),
    )(class_grad, ids, scores)
    payload, grad_late = lax.optimization_barrier((payload, grad_out))
    shared_part = lax.dot_general(
        shared_weight, grad_late, (((1,), (1,)), ((), ())), preferred_element_type=jnp.float32
    )
    shared_part = swap_halves(shared_part.reshape(local_count, -1, tokens), local_count, 1)
    shared_part = swap_halves(shared_part, local_count, 2).astype(jnp.bfloat16)
    received = lax.all_to_all(
        payload.reshape(node_count, capacity, padded), "node", split_axis=0, concat_axis=0, tiled=True
    ).reshape(rows_total, padded)
    received, shared_part = lax.optimization_barrier((received, shared_part))

    half = 4 * LANES
    lower, upper = received[:, :half], received[:, half:class_width]
    right = [(z, (z + 1) % local_count) for z in range(local_count)]
    left = [(z, (z - 1) % local_count) for z in range(local_count)]
    by_class = down_weight.reshape(quarter_width, -1, CLASSES, slice_width)
    by_class = by_class.transpose(2, 0, 1, 3).reshape(CLASSES, quarter_width, class_width)

    def partial(rows, shift, part):
        own_class = (lax.axis_index("local") + shift) % CLASSES
        weight = lax.dynamic_index_in_dim(by_class, own_class, 0, keepdims=False)
        weight = weight[:, half:] if part else weight[:, :half]
        return lax.dot_general(rows, weight, (((1,), (1,)), ((), ())), preferred_element_type=jnp.float32)

    lower_left = lax.ppermute(lower, "local", right)
    upper_right = lax.ppermute(upper, "local", left)
    hidden_grad = partial(lower, 0, 0) + partial(upper, 0, 1)
    lower, upper, hidden_grad = lax.optimization_barrier((lower, upper, hidden_grad))
    upper_left = lax.ppermute(upper, "local", right)
    lower_right = lax.ppermute(lower, "local", left)
    lower_far = lax.ppermute(lower_left, "local", right)
    upper_far = lax.ppermute(upper_right, "local", left)
    hidden_grad = hidden_grad + partial(lower_left, CLASSES - 1, 0)
    hidden_grad = hidden_grad + partial(upper_right, 1, 1)
    hidden_grad = hidden_grad + partial(upper_left, CLASSES - 1, 1)
    hidden_grad = hidden_grad + partial(lower_right, 1, 0)
    hidden_grad = hidden_grad + partial(lower_far, 2, 0)
    hidden_grad = hidden_grad + partial(upper_far, 2, 1)
    gate_column = lax.dynamic_slice_in_dim(received, class_width + own_expert, 1, 1).astype(jnp.float32)
    expert_grad = (
        (gate_column * hidden_grad).astype(jnp.bfloat16).reshape(1, rows_total, quarter_width)
    )
    slot_dots = jnp.sum(hidden_grad * saved_hidden[0].astype(jnp.float32), axis=1)

    returned = lax.all_to_all(
        slot_dots.reshape(node_count, 1, capacity), "node", split_axis=0, concat_axis=0, tiled=True
    )
    height = shared_part.shape[1]
    extra = (3 * rows_total // LANES + 15) // 16 * 16
    spread = pl.pallas_call(
        lambda *refs: spread_kernel(capacity, *refs),
        out_shape=jax.ShapeDtypeStruct((local_count, height + extra, tokens), jnp.bfloat16),
        in_specs=[vmem] * 2,
        out_specs=vmem,
        compiler_params=small,
    )(returned, shared_part)
    parts = lax.all_to_all(spread, "local", split_axis=0, concat_axis=0, tiled=True)
    router_grad, shared_grad = pl.pallas_call(
        lambda *refs: router_kernel(capacity, *refs),
        out_shape=(
            jax.ShapeDtypeStruct(scores.shape, jnp.float32),
            jax.ShapeDtypeStruct((4 * height, tokens), jnp.bfloat16),
        ),
        in_specs=[vmem] * 4,
        out_specs=(vmem, vmem),
        compiler_params=small,
    )(parts, select, ids, scores)
    return (expert_grad, router_grad.T, shared_grad)


def solution(mesh):
    return jax.shard_map(
        body,
        mesh=mesh,
        in_specs=(
            P("node", "local"),
            P("node", None),
            P("node", None),
            P("node", None, "local"),
            P(("node", "local"), None),
            P(None, "local"),
        ),
        out_specs=(P("node", None, "local"), P("node", None), P("local", "node")),
        check_vma=False,
    )
```

```python
import jax
import jax.numpy as jnp
from jax import lax
from jax.experimental import pallas as pl
from jax.experimental.pallas import tpu as pltpu
from jax.sharding import PartitionSpec as P

EXP_NODE = 4
LANES = 128
CLASSES = 4
KERNEL_VMEM = 8 << 20

route_scale = 2.5


def iota(shape, dim):
    return lax.broadcasted_iota(jnp.int32, shape, dim)


def as_bf16(mask):
    return mask.astype(jnp.float32).astype(jnp.bfloat16)


def across(left, right):
    return lax.dot_general(left, right, (((1,), (1,)), ((), ())), preferred_element_type=jnp.float32)


def pieces(value):
    high = value.astype(jnp.bfloat16)
    rest = value - high.astype(jnp.float32)
    middle = rest.astype(jnp.bfloat16)
    low = (rest - middle.astype(jnp.float32)).astype(jnp.bfloat16)
    return high, middle, low


def exact_dot(left, right):
    high, middle, low = (jnp.dot(piece, right, preferred_element_type=jnp.float32) for piece in pieces(left))
    return high + middle + low


def route_kernel(capacity, grad_ref, ids_ref, scores_ref, payload_ref, select_ref):
    width, tokens = grad_ref.shape
    rows, padded = payload_ref.shape
    top = ids_ref.shape[0]
    experts = rows // capacity * EXP_NODE
    ids = ids_ref[...]
    scores = scores_ref[...]
    group = iota((rows, tokens), 0) // capacity
    picked = ids // EXP_NODE
    hits = group == picked[0:1, :]
    for k in range(1, top):
        hits = hits | (group == picked[k:k + 1, :])
    hot = hits.astype(jnp.float32)
    before = as_bf16(iota((tokens, tokens), 0) < iota((tokens, tokens), 1))
    rank = jnp.dot(hot.astype(jnp.bfloat16), before, preferred_element_type=jnp.float32)
    slot = (iota((rows, tokens), 0) % capacity).astype(jnp.float32)
    select = jnp.where(rank == slot, hot, 0.0).astype(jnp.bfloat16)
    select_ref[...] = select
    totals = jnp.sum(scores, axis=0, keepdims=True)
    weights = (route_scale * scores / totals).astype(jnp.bfloat16).astype(jnp.float32)
    expert = iota((experts, tokens), 0)
    spread = jnp.zeros((experts, tokens), jnp.float32)
    for k in range(top):
        spread = spread + jnp.where(expert == ids[k:k + 1, :], weights[k:k + 1, :], 0.0)
    payload_ref[:, :width] = across(select, grad_ref[...]).astype(payload_ref.dtype)
    gates = across(select, spread.astype(jnp.bfloat16))
    own = iota((rows, experts), 0) // capacity == iota((rows, experts), 1) // EXP_NODE
    place = iota((experts, padded - width), 0) % EXP_NODE == iota((experts, padded - width), 1)
    gates = jnp.dot(
        jnp.where(own, gates, 0.0).astype(jnp.bfloat16), as_bf16(place), preferred_element_type=jnp.float32
    )
    payload_ref[:, width:] = gates.astype(payload_ref.dtype)


def spread_kernel(capacity, score_ref, shared_ref, out_ref):
    groups = score_ref.shape[0]
    copies, height, lanes = shared_ref.shape
    score = score_ref[...].reshape(groups, score_ref.shape[2])
    held = lanes // capacity
    repeat = as_bf16(iota((capacity, lanes), 0) == iota((capacity, lanes), 1) % capacity)
    own = iota((groups, lanes), 0) % held == iota((groups, lanes), 1) // capacity
    lines = []
    for piece in pieces(score):
        tiled = jnp.where(own, jnp.dot(piece, repeat, preferred_element_type=jnp.float32), 0.0)
        for j in range(groups // held):
            lines.append(jnp.sum(tiled[j * held:(j + 1) * held, :], axis=0, keepdims=True))
    filler = out_ref.shape[1] - height - len(lines)
    lines.append(jnp.zeros((filler, lanes), jnp.float32))
    flat = jnp.concatenate(lines, axis=0).astype(jnp.bfloat16)
    for z in range(copies):
        out_ref[z, :height, :] = shared_ref[z]
        out_ref[z, height:, :] = flat


def router_kernel(capacity, parts_ref, select_ref, ids_ref, scores_ref, out_ref, shared_ref):
    copies, _, lanes = parts_ref.shape
    height = shared_ref.shape[0] // 4
    rows, tokens = select_ref.shape
    lines = rows // lanes
    top = ids_ref.shape[0]
    shares = copies // EXP_NODE
    held = lanes // capacity
    for first in range(4):
        shared = parts_ref[first, :height, :].astype(jnp.float32)
        for z in range(first + 4, copies, 4):
            shared = shared + parts_ref[z, :height, :].astype(jnp.float32)
        start = (first % 2 * 2 + first // 2) * height
        shared_ref[start:start + height, :] = shared.astype(shared_ref.dtype)
    ids = ids_ref[...]
    scores = scores_ref[...]
    fold = iota((held, lanes), 0) == iota((held, lanes), 1) // capacity
    score = []
    for c in range(EXP_NODE):
        total = jnp.zeros((lines, lanes), jnp.float32)
        for q in range(shares):
            sent = parts_ref[c * shares + q, height:, :].astype(jnp.float32)
            total = total + (sent[:lines] + sent[lines:2 * lines] + sent[2 * lines:3 * lines])
        score.append(total)
    pick = iota((top, tokens), 0)
    line = iota((EXP_NODE * held, tokens), 0)
    expert = line % held * EXP_NODE + line // held
    contrib = jnp.zeros((top, tokens), jnp.float32)
    for j in range(lines):
        left = jnp.concatenate([jnp.where(fold, score[c][j:j + 1, :], 0.0) for c in range(EXP_NODE)], axis=0)
        found = exact_dot(left, select_ref[j * lanes:(j + 1) * lanes, :])
        for k in range(top):
            mine = jnp.where(expert + j * held * EXP_NODE == ids[k:k + 1, :], found, 0.0)
            contrib = contrib + jnp.where(pick == k, jnp.sum(mine, axis=0, keepdims=True), 0.0)
    totals = jnp.sum(scores, axis=0, keepdims=True)
    mean_term = jnp.sum(scores * contrib, axis=0, keepdims=True) / totals
    out_ref[...] = route_scale / totals * (contrib - mean_term) * scores * (1.0 - scores)


def swap_halves(part, count, bit):
    kept = lax.axis_index("local") // bit % 2
    halves = part.reshape(count, 2, -1, part.shape[2])
    given = lax.dynamic_index_in_dim(halves, 1 - kept, 1, keepdims=False).astype(jnp.bfloat16)
    swapped = lax.ppermute(given, "local", [(z, z ^ bit) for z in range(count)])
    return lax.dynamic_index_in_dim(halves, kept, 1, keepdims=False) + swapped.astype(jnp.float32)


def body(grad_out, expert_ids, gate_scores, saved_hidden, down_weight, shared_weight):
    node_count = lax.axis_size("node")
    local_count = lax.axis_size("local")
    rows_total = saved_hidden.shape[1]
    capacity = rows_total // node_count
    tokens, slice_width = grad_out.shape
    quarter_width = down_weight.shape[0]
    share_count = local_count // EXP_NODE
    class_width = slice_width * local_count // CLASSES
    padded = class_width + LANES
    own_expert = lax.axis_index("local") // share_count
    ids = expert_ids.T
    scores = gate_scores.T
    vmem = pl.BlockSpec(memory_space=pltpu.VMEM)
    small = pltpu.CompilerParams(vmem_limit_bytes=KERNEL_VMEM)

    groups = [list(range(j, local_count, CLASSES)) for j in range(CLASSES)]
    class_grad = lax.all_gather(grad_out.T, "local", axis=0, tiled=True, axis_index_groups=groups)
    payload, select = pl.pallas_call(
        lambda *refs: route_kernel(capacity, *refs),
        out_shape=(
            jax.ShapeDtypeStruct((rows_total, padded), jnp.bfloat16),
            jax.ShapeDtypeStruct((rows_total, tokens), jnp.bfloat16),
        ),
        compiler_params=pltpu.CompilerParams(vmem_limit_bytes=2 * KERNEL_VMEM),
    )(class_grad, ids, scores)
    payload, grad_late = lax.optimization_barrier((payload, grad_out))
    shared_part = lax.dot_general(
        shared_weight, grad_late, (((1,), (1,)), ((), ())), preferred_element_type=jnp.float32
    )
    shared_part = swap_halves(shared_part.reshape(local_count, -1, tokens), local_count, 1)
    shared_part = swap_halves(shared_part, local_count, 2).astype(jnp.bfloat16)
    received = lax.all_to_all(
        payload.reshape(node_count, capacity, padded), "node", split_axis=0, concat_axis=0, tiled=True
    ).reshape(rows_total, padded)
    received, shared_part = lax.optimization_barrier((received, shared_part))

    half = 4 * LANES
    lower, upper = received[:, :half], received[:, half:]
    right = [(z, (z + 1) % local_count) for z in range(local_count)]
    left = [(z, (z - 1) % local_count) for z in range(local_count)]
    by_class = down_weight.reshape(quarter_width, -1, CLASSES, slice_width)
    by_class = by_class.transpose(2, 0, 1, 3).reshape(CLASSES, quarter_width, class_width)
    by_class = jnp.pad(by_class, ((0, 0), (0, 0), (0, padded - class_width)))

    def partial(rows, shift, part):
        own_class = (lax.axis_index("local") + shift) % CLASSES
        weight = lax.dynamic_index_in_dim(by_class, own_class, 0, keepdims=False)
        weight = weight[:, half:] if part else weight[:, :half]
        return lax.dot_general(rows, weight, (((1,), (1,)), ((), ())), preferred_element_type=jnp.float32)

    lower_left = lax.ppermute(lower, "local", right)
    upper_right = lax.ppermute(upper, "local", left)
    hidden_grad = partial(lower, 0, 0) + partial(upper, 0, 1)
    lower, upper, hidden_grad = lax.optimization_barrier((lower, upper, hidden_grad))
    upper_left = lax.ppermute(upper, "local", right)
    lower_right = lax.ppermute(lower, "local", left)
    lower_far = lax.ppermute(lower_left, "local", right)
    upper_far = lax.ppermute(upper_right, "local", left)
    hidden_grad = hidden_grad + partial(lower_left, CLASSES - 1, 0)
    hidden_grad = hidden_grad + partial(upper_right, 1, 1)
    hidden_grad = hidden_grad + partial(upper_left, CLASSES - 1, 1)
    hidden_grad = hidden_grad + partial(lower_right, 1, 0)
    hidden_grad = hidden_grad + partial(lower_far, 2, 0)
    hidden_grad = hidden_grad + partial(upper_far, 2, 1)
    gate_column = lax.dynamic_slice_in_dim(received, class_width + own_expert, 1, 1).astype(jnp.float32)
    expert_grad = (
        (gate_column * hidden_grad).astype(jnp.bfloat16).reshape(1, rows_total, quarter_width)
    )
    slot_dots = jnp.sum(hidden_grad * saved_hidden[0].astype(jnp.float32), axis=1)

    returned = lax.all_to_all(
        slot_dots.reshape(node_count, 1, capacity), "node", split_axis=0, concat_axis=0, tiled=True
    )
    height = shared_part.shape[1]
    extra = (3 * rows_total // LANES + 15) // 16 * 16
    spread = pl.pallas_call(
        lambda *refs: spread_kernel(capacity, *refs),
        out_shape=jax.ShapeDtypeStruct((local_count, height + extra, tokens), jnp.bfloat16),
        in_specs=[vmem] * 2,
        out_specs=vmem,
        compiler_params=small,
    )(returned, shared_part)
    parts = lax.all_to_all(spread, "local", split_axis=0, concat_axis=0, tiled=True)
    router_grad, shared_grad = pl.pallas_call(
        lambda *refs: router_kernel(capacity, *refs),
        out_shape=(
            jax.ShapeDtypeStruct(scores.shape, jnp.float32),
            jax.ShapeDtypeStruct((4 * height, tokens), jnp.bfloat16),
        ),
        in_specs=[vmem] * 4,
        out_specs=(vmem, vmem),
        compiler_params=small,
    )(parts, select, ids, scores)
    return (expert_grad, router_grad.T, shared_grad)


def solution(mesh):
    return jax.shard_map(
        body,
        mesh=mesh,
        in_specs=(
            P("node", "local"),
            P("node", None),
            P("node", None),
            P("node", None, "local"),
            P(("node", "local"), None),
            P(None, "local"),
        ),
        out_specs=(P("node", None, "local"), P("node", None), P("local", "node")),
        check_vma=False,
    )
```

```python
import jax
import jax.numpy as jnp
from jax import lax
from jax.experimental import pallas as pl
from jax.experimental.pallas import tpu as pltpu
from jax.sharding import PartitionSpec as P

EXP_NODE = 4
LANES = 128
CLASSES = 4
KERNEL_VMEM = 8 << 20

route_scale = 2.5


def iota(shape, dim):
    return lax.broadcasted_iota(jnp.int32, shape, dim)


def as_bf16(mask):
    return mask.astype(jnp.float32).astype(jnp.bfloat16)


def across(left, right):
    return lax.dot_general(left, right, (((1,), (1,)), ((), ())), preferred_element_type=jnp.float32)


def pieces(value):
    high = value.astype(jnp.bfloat16)
    rest = value - high.astype(jnp.float32)
    middle = rest.astype(jnp.bfloat16)
    low = (rest - middle.astype(jnp.float32)).astype(jnp.bfloat16)
    return high, middle, low


def exact_dot(left, right):
    high, middle, low = (jnp.dot(piece, right, preferred_element_type=jnp.float32) for piece in pieces(left))
    return high + middle + low


def route_kernel(capacity, grad_ref, ids_ref, scores_ref, payload_ref, select_ref):
    width, tokens = grad_ref.shape
    rows, padded = payload_ref.shape
    top = ids_ref.shape[0]
    experts = rows // capacity * EXP_NODE
    ids = ids_ref[...]
    scores = scores_ref[...]
    group = iota((rows, tokens), 0) // capacity
    picked = ids // EXP_NODE
    hits = group == picked[0:1, :]
    for k in range(1, top):
        hits = hits | (group == picked[k:k + 1, :])
    hot = hits.astype(jnp.float32)
    before = as_bf16(iota((tokens, tokens), 0) < iota((tokens, tokens), 1))
    rank = jnp.dot(hot.astype(jnp.bfloat16), before, preferred_element_type=jnp.float32)
    slot = (iota((rows, tokens), 0) % capacity).astype(jnp.float32)
    select = jnp.where(rank == slot, hot, 0.0).astype(jnp.bfloat16)
    select_ref[...] = select
    totals = jnp.sum(scores, axis=0, keepdims=True)
    weights = (route_scale * scores / totals).astype(jnp.bfloat16).astype(jnp.float32)
    expert = iota((experts, tokens), 0)
    spread = jnp.zeros((experts, tokens), jnp.float32)
    for k in range(top):
        spread = spread + jnp.where(expert == ids[k:k + 1, :], weights[k:k + 1, :], 0.0)
    payload_ref[:, :width] = across(select, grad_ref[...]).astype(payload_ref.dtype)
    gates = across(select, spread.astype(jnp.bfloat16))
    own = iota((rows, experts), 0) // capacity == iota((rows, experts), 1) // EXP_NODE
    place = iota((experts, padded - width), 0) % EXP_NODE == iota((experts, padded - width), 1)
    gates = jnp.dot(
        jnp.where(own, gates, 0.0).astype(jnp.bfloat16), as_bf16(place), preferred_element_type=jnp.float32
    )
    payload_ref[:, width:] = gates.astype(payload_ref.dtype)


def spread_kernel(capacity, score_ref, shared_ref, out_ref):
    groups = score_ref.shape[0]
    copies, height, lanes = shared_ref.shape
    score = score_ref[...].reshape(groups, score_ref.shape[2])
    held = lanes // capacity
    repeat = as_bf16(iota((capacity, lanes), 0) == iota((capacity, lanes), 1) % capacity)
    own = iota((groups, lanes), 0) % held == iota((groups, lanes), 1) // capacity
    lines = []
    for piece in pieces(score):
        tiled = jnp.where(own, jnp.dot(piece, repeat, preferred_element_type=jnp.float32), 0.0)
        for j in range(groups // held):
            lines.append(jnp.sum(tiled[j * held:(j + 1) * held, :], axis=0, keepdims=True))
    filler = out_ref.shape[1] - height - len(lines)
    lines.append(jnp.zeros((filler, lanes), jnp.float32))
    flat = jnp.concatenate(lines, axis=0).astype(jnp.bfloat16)
    for z in range(copies):
        out_ref[z, :height, :] = shared_ref[z]
        out_ref[z, height:, :] = flat


def router_kernel(capacity, parts_ref, select_ref, ids_ref, scores_ref, out_ref, shared_ref):
    copies, _, lanes = parts_ref.shape
    height = shared_ref.shape[0] // 4
    rows, tokens = select_ref.shape
    lines = rows // lanes
    top = ids_ref.shape[0]
    shares = copies // EXP_NODE
    held = lanes // capacity
    for first in range(4):
        shared = parts_ref[first, :height, :].astype(jnp.float32)
        for z in range(first + 4, copies, 4):
            shared = shared + parts_ref[z, :height, :].astype(jnp.float32)
        start = (first % 2 * 2 + first // 2) * height
        shared_ref[start:start + height, :] = shared.astype(shared_ref.dtype)
    ids = ids_ref[...]
    scores = scores_ref[...]
    fold = iota((held, lanes), 0) == iota((held, lanes), 1) // capacity
    score = []
    for c in range(EXP_NODE):
        total = jnp.zeros((lines, lanes), jnp.float32)
        for q in range(shares):
            sent = parts_ref[c * shares + q, height:, :].astype(jnp.float32)
            total = total + (sent[:lines] + sent[lines:2 * lines] + sent[2 * lines:3 * lines])
        score.append(total)
    pick = iota((top, tokens), 0)
    line = iota((EXP_NODE * held, tokens), 0)
    expert = line % held * EXP_NODE + line // held
    contrib = jnp.zeros((top, tokens), jnp.float32)
    for j in range(lines):
        left = jnp.concatenate([jnp.where(fold, score[c][j:j + 1, :], 0.0) for c in range(EXP_NODE)], axis=0)
        found = exact_dot(left, select_ref[j * lanes:(j + 1) * lanes, :])
        for k in range(top):
            mine = jnp.where(expert + j * held * EXP_NODE == ids[k:k + 1, :], found, 0.0)
            contrib = contrib + jnp.where(pick == k, jnp.sum(mine, axis=0, keepdims=True), 0.0)
    totals = jnp.sum(scores, axis=0, keepdims=True)
    mean_term = jnp.sum(scores * contrib, axis=0, keepdims=True) / totals
    out_ref[...] = route_scale / totals * (contrib - mean_term) * scores * (1.0 - scores)


def swap_halves(part, count, bit):
    kept = lax.axis_index("local") // bit % 2
    halves = part.reshape(count, 2, -1, part.shape[2])
    given = lax.dynamic_index_in_dim(halves, 1 - kept, 1, keepdims=False).astype(jnp.bfloat16)
    swapped = lax.ppermute(given, "local", [(z, z ^ bit) for z in range(count)])
    return lax.dynamic_index_in_dim(halves, kept, 1, keepdims=False) + swapped.astype(jnp.float32)


def body(grad_out, expert_ids, gate_scores, saved_hidden, down_weight, shared_weight):
    node_count = lax.axis_size("node")
    local_count = lax.axis_size("local")
    rows_total = saved_hidden.shape[1]
    capacity = rows_total // node_count
    tokens, slice_width = grad_out.shape
    quarter_width = down_weight.shape[0]
    share_count = local_count // EXP_NODE
    class_width = slice_width * local_count // CLASSES
    padded = class_width + LANES
    own_expert = lax.axis_index("local") // share_count
    ids = expert_ids.T
    scores = gate_scores.T
    vmem = pl.BlockSpec(memory_space=pltpu.VMEM)
    small = pltpu.CompilerParams(vmem_limit_bytes=KERNEL_VMEM)

    groups = [list(range(j, local_count, CLASSES)) for j in range(CLASSES)]
    class_grad = lax.all_gather(grad_out.T, "local", axis=0, tiled=True, axis_index_groups=groups)
    payload, select = pl.pallas_call(
        lambda *refs: route_kernel(capacity, *refs),
        out_shape=(
            jax.ShapeDtypeStruct((rows_total, padded), jnp.bfloat16),
            jax.ShapeDtypeStruct((rows_total, tokens), jnp.bfloat16),
        ),
        compiler_params=pltpu.CompilerParams(vmem_limit_bytes=2 * KERNEL_VMEM),
    )(class_grad, ids, scores)
    payload, grad_late = lax.optimization_barrier((payload, grad_out))
    shared_part = lax.dot_general(
        shared_weight, grad_late, (((1,), (1,)), ((), ())), preferred_element_type=jnp.float32
    )
    shared_part = swap_halves(shared_part.reshape(local_count, -1, tokens), local_count, 1)
    shared_part = swap_halves(shared_part, local_count, 2).astype(jnp.bfloat16)
    received = lax.all_to_all(
        payload.reshape(node_count, capacity, padded), "node", split_axis=0, concat_axis=0, tiled=True
    ).reshape(rows_total, padded)
    received, shared_part = lax.optimization_barrier((received, shared_part))

    half = rows_total // 2
    lower, upper = received[:half, :class_width], received[half:, :class_width]
    right = [(z, (z + 1) % local_count) for z in range(local_count)]
    left = [(z, (z - 1) % local_count) for z in range(local_count)]
    by_class = down_weight.reshape(quarter_width, -1, CLASSES, slice_width)
    by_class = by_class.transpose(2, 0, 1, 3).reshape(CLASSES, quarter_width, class_width)

    def partial(rows, shift):
        own_class = (lax.axis_index("local") + shift) % CLASSES
        weight = lax.dynamic_index_in_dim(by_class, own_class, 0, keepdims=False)
        return lax.dot_general(rows, weight, (((1,), (1,)), ((), ())), preferred_element_type=jnp.float32)

    lower_left = lax.ppermute(lower, "local", right)
    upper_right = lax.ppermute(upper, "local", left)
    lower_grad, upper_grad = partial(lower, 0), partial(upper, 0)
    lower, upper, lower_grad, upper_grad = lax.optimization_barrier((lower, upper, lower_grad, upper_grad))
    upper_left = lax.ppermute(upper, "local", right)
    lower_right = lax.ppermute(lower, "local", left)
    lower_far = lax.ppermute(lower_left, "local", right)
    upper_far = lax.ppermute(upper_right, "local", left)
    lower_grad = lower_grad + partial(lower_left, CLASSES - 1) + partial(lower_right, 1)
    upper_grad = upper_grad + partial(upper_right, 1) + partial(upper_left, CLASSES - 1)
    lower_grad = lower_grad + partial(lower_far, 2)
    upper_grad = upper_grad + partial(upper_far, 2)
    gate_column = lax.dynamic_slice_in_dim(received, class_width + own_expert, 1, 1).astype(jnp.float32)
    saved = saved_hidden[0].astype(jnp.float32)
    experts, dots = [], []
    for start, hidden_grad in ((0, lower_grad), (half, upper_grad)):
        span = slice(start, start + half)
        experts.append((gate_column[span] * hidden_grad).astype(jnp.bfloat16))
        dots.append(jnp.sum(hidden_grad * saved[span], axis=1))
    expert_grad = jnp.concatenate(experts, axis=0).reshape(1, rows_total, quarter_width)
    slot_dots = jnp.concatenate(dots, axis=0)

    returned = lax.all_to_all(
        slot_dots.reshape(node_count, 1, capacity), "node", split_axis=0, concat_axis=0, tiled=True
    )
    height = shared_part.shape[1]
    extra = (3 * rows_total // LANES + 15) // 16 * 16
    spread = pl.pallas_call(
        lambda *refs: spread_kernel(capacity, *refs),
        out_shape=jax.ShapeDtypeStruct((local_count, height + extra, tokens), jnp.bfloat16),
        in_specs=[vmem] * 2,
        out_specs=vmem,
        compiler_params=small,
    )(returned, shared_part)
    parts = lax.all_to_all(spread, "local", split_axis=0, concat_axis=0, tiled=True)
    router_grad, shared_grad = pl.pallas_call(
        lambda *refs: router_kernel(capacity, *refs),
        out_shape=(
            jax.ShapeDtypeStruct(scores.shape, jnp.float32),
            jax.ShapeDtypeStruct((4 * height, tokens), jnp.bfloat16),
        ),
        in_specs=[vmem] * 4,
        out_specs=(vmem, vmem),
        compiler_params=small,
    )(parts, select, ids, scores)
    return (expert_grad, router_grad.T, shared_grad)


def solution(mesh):
    return jax.shard_map(
        body,
        mesh=mesh,
        in_specs=(
            P("node", "local"),
            P("node", None),
            P("node", None),
            P("node", None, "local"),
            P(("node", "local"), None),
            P(None, "local"),
        ),
        out_specs=(P("node", None, "local"), P("node", None), P("local", "node")),
        check_vma=False,
    )
```
